32 devices in a mesh: gx: 8 (over z, y), gy: 2 (over x), gz: 2 (over core).
Axes of the slice: x: 2, y: 2, z: 4, core: 2. Of those that a mesh axis runs over, the one named last changes fastest.
Arguments:
- tokens: bfloat16 [64, 32, 128, 128], P('gx', 'gy', 'gz'), may hold values from -6 to 6
- w_qkv: bfloat16 [128, 384], replicated, may hold values from -0.5 to 0.5
- w_out: bfloat16 [128, 128], replicated, may hold values from -0.5 to 0.5
- w_gate_up: bfloat16 [128, 1024], replicated, may hold values from -0.5 to 0.5
- w_down: bfloat16 [512, 128], replicated, may hold values from -0.25 to 0.25
Outputs:
- updated: bfloat16 [64, 32, 128, 128], P('gx', 'gy', 'gz')
The draws below stay inside these ranges and needn't reach their ends.
All inputs are finite; a program needn't handle non-finite values.
Results may differ from the reference program's by a relative error of at most 0.014.
Values may be sent and summed in bfloat16 or wider, within the bound.
A program may use at most 64 MiB of HBM per device.

```python
import math
import jax
import jax.numpy as jnp
from jax import lax

C = 128
HEADS = 8
FF = 512
LINE_X = 64
LINE_Y = 32
LINE_Z = 128


def block_scale(rng, dims, shards, least, top_value):
    level = 1.0
    for position, shards_of in shards:
        draws = jax.random.uniform(jax.random.fold_in(jax.random.fold_in(rng, 6), position), (shards_of,), jnp.float32, least / len(shards), top_value / len(shards))
        level = level * jnp.repeat(jnp.exp(draws), dims[position] // shards_of).reshape((-1,) + (1,) * (len(dims) - 1 - position))
    return level


def scatter_about(stream_key, extent, deviation, limit, cuts=(), dtype=jnp.bfloat16):
    array = deviation * jax.random.normal(stream_key, extent, jnp.float32)
    if cuts:
        array = array * block_scale(stream_key, extent, cuts, -0.22, 0.18)
    return jnp.clip(array, -limit, limit).astype(dtype)


def setup_inputs(seed: int = 0) -> dict:
    streams_of = jax.random.split(jax.random.key(seed), 6)
    tokens = scatter_about(streams_of[0], (LINE_X, LINE_Y, LINE_Z, C), 1.0, 6.0, ((0, 8), (1, 2), (2, 2)))
    w_qkv = scatter_about(streams_of[1], (C, 3 * C), C ** -0.5, 0.5)
    w_out = scatter_about(streams_of[2], (C, C), C ** -0.5, 0.5)
    w_gate_up = scatter_about(streams_of[3], (C, 2 * FF), C ** -0.5, 0.5)
    w_down = scatter_about(streams_of[4], (FF, C), FF ** -0.5, 0.25)
    return {"tokens": tokens, "w_qkv": w_qkv, "w_out": w_out, "w_gate_up": w_gate_up, "w_down": w_down}


EPS = 1e-05

def norm_rows(values):
    mean = lax.optimization_barrier(jnp.mean(values, axis=-1, keepdims=True))
    centred = values - mean
    spread = lax.optimization_barrier(jnp.mean(centred * centred, axis=-1, keepdims=True))
    return centred * lax.rsqrt(spread + EPS)

def unit_scale(values):
    return values * lax.rsqrt(jnp.mean(values * values) + 1e-06)

def make_kernel(pooled, length):
    width = pooled.shape[1] // 2
    head_dim = width // HEADS
    query = unit_scale(pooled[:, :width]).reshape(length, HEADS, head_dim)
    key_part = unit_scale(pooled[:, width:]).reshape(length, HEADS, head_dim)
    kernel = jnp.einsum('ahd,bhd->hab', query, key_part, precision=lax.Precision.HIGHEST)
    return (kernel / math.sqrt(head_dim * length)).astype(jnp.bfloat16)

def apply_first(kernel, block):
    length = block.shape[0]
    split = block.reshape(length, -1, HEADS, block.shape[-1] // HEADS).astype(jnp.float32)
    mixed = jnp.einsum('hab,bmhd->amhd', kernel.astype(jnp.float32), split)
    return mixed.reshape(block.shape)

def apply_second(kernel, block):
    split = block.reshape(block.shape[0], block.shape[1], HEADS, block.shape[-1] // HEADS).astype(jnp.float32)
    mixed = jnp.einsum('hab,ybhd->yahd', kernel.astype(jnp.float32), split)
    return mixed.reshape(block.shape)

def finish(mixed, slab, w_out, w_gate_up, w_down):
    width = slab.shape[-1]
    resid = slab.astype(jnp.float32).reshape(-1, width) + jnp.dot(mixed.reshape(-1, width), w_out, preferred_element_type=jnp.float32)
    inner = norm_rows(resid).astype(jnp.bfloat16)
    both = jnp.dot(inner, w_gate_up, preferred_element_type=jnp.float32)
    hidden = (jax.nn.gelu(both[:, :FF]) * both[:, FF:]).astype(jnp.bfloat16)
    result = resid + jnp.dot(hidden, w_down, preferred_element_type=jnp.float32)
    return result.astype(jnp.bfloat16).reshape(slab.shape)

def reference(tokens, w_qkv, w_out, w_gate_up, w_down):
    width = tokens.shape[-1]

    def project(slab):
        normed = norm_rows(slab.astype(jnp.float32)).astype(jnp.bfloat16)
        qkv = jnp.dot(normed.reshape(-1, width), w_qkv, preferred_element_type=jnp.float32)
        qkv = qkv.reshape(slab.shape[0], slab.shape[1], 3 * width)
        both = qkv[..., :2 * width]
        return (qkv[..., 2 * width:].astype(jnp.bfloat16), lax.optimization_barrier(jnp.sum(both, axis=(0, 1))), lax.optimization_barrier(jnp.sum(both, axis=1)), lax.optimization_barrier(jnp.sum(both, axis=0)))
    value, pool_x, part_y, part_z = lax.map(project, tokens)
    kernel_x = make_kernel(pool_x, LINE_X)
    kernel_y = make_kernel(lax.optimization_barrier(jnp.sum(part_y, axis=0)), LINE_Y)
    kernel_z = make_kernel(lax.optimization_barrier(jnp.sum(part_z, axis=0)), LINE_Z)

    def mix_x(block):
        return apply_first(kernel_x, block).astype(jnp.bfloat16)
    after_x = jnp.transpose(lax.map(mix_x, jnp.transpose(value, (1, 0, 2, 3))), (1, 0, 2, 3))

    def rest(pair):
        block, slab = pair
        after_y = apply_first(kernel_y, block).astype(jnp.bfloat16)
        mixed = apply_second(kernel_z, after_y).astype(jnp.bfloat16)
        return finish(mixed, slab, w_out, w_gate_up, w_down)
    return lax.map(rest, (after_x, tokens))
```

```python
import functools
import math

import jax
import jax.numpy as jnp
from jax import lax
from jax.experimental import pallas as pl
from jax.experimental.pallas import tpu as pltpu
from jax.sharding import PartitionSpec as P

HEADS = 8
EPS = 1e-05
VMEM_LIMIT = 56 * 1024 * 1024
F32 = jnp.float32
BF16 = jnp.bfloat16


def dot(a, b):
    return jnp.dot(a, b, preferred_element_type=F32)


def averaging(width):
    return jnp.full((width, width), 1.0 / width, BF16)


def head_mask(width, rank):
    shape = (HEADS, 1, width)
    lane = lax.broadcasted_iota(jnp.int32, shape, 2)
    return lane // rank == lax.broadcasted_iota(jnp.int32, shape, 0)


def spread_lanes(coef, out_ref, rank):
    width = coef.shape[-1]
    row = lax.broadcasted_iota(jnp.int32, (width, width), 0)
    lane = lax.broadcasted_iota(jnp.int32, (width, width), 1)
    same = row // rank == lane // rank
    for d in range(rank):
        pick = jnp.where(same & (row % rank == d), 1.0, 0.0).astype(BF16)
        out_ref[:, d, :] = dot(coef.astype(BF16), pick)


def project_kernel(lines, tok_ref, wv_ref, val_ref, pool_ref):
    step = pl.program_id(0)
    _, ny, nz, width = tok_ref.shape
    nx = pl.num_programs(0)

    @pl.when(step == 0)
    def _():
        pool_ref[...] = jnp.zeros_like(pool_ref)

    avg = averaging(width)
    tok = tok_ref[...].reshape(ny * nz, width)
    cent = tok.astype(F32) - dot(tok, avg)
    var = dot((cent * cent).astype(BF16), avg)
    normed = (cent * lax.rsqrt(var + EPS)).astype(BF16)
    val_ref[...] = dot(normed, wv_ref[...]).astype(BF16).reshape(val_ref.shape)
    full = normed.astype(F32).reshape(ny, nz, width)
    by_y = jnp.sum(full, axis=1)
    gx, gy, gz = (lax.axis_index(a) for a in ("gx", "gy", "gz"))
    rows_y = pl.ds(pl.multiple_of(lines[0] + gy * ny, 8), ny)
    rows_z = pl.ds(pl.multiple_of(lines[0] + lines[1] + gz * nz, 8), nz)
    pool_ref[pl.ds(gx * nx + step, 1), :] = jnp.sum(by_y, axis=0, keepdims=True)
    pool_ref[rows_y, :] += by_y
    pool_ref[rows_z, :] += jnp.sum(full, axis=0)


def coefficients(lines, pool, w_qk, out_ref):
    width = pool.shape[-1]
    rank = width // HEADS
    both = jnp.dot(pool, w_qk.astype(F32), precision=lax.Precision.HIGHEST)
    start = 0
    for length in lines:
        for part in range(2):
            cut = both[start : start + length, part * width : (part + 1) * width]
            total = jnp.sum(jnp.sum(cut * cut, axis=0, keepdims=True), axis=1, keepdims=True)
            unit = cut * lax.rsqrt(total / (length * width) + 1e-06)
            if part == 0:
                unit = unit * (1.0 / math.sqrt(rank * length))
            out_ref[start : start + length, part * width : (part + 1) * width] = unit
        start += length


def compress_kernel(lines, pool_ref, wqk_ref, val_ref, out_ref, coef_ref, key_y, key_z, state):
    _, ny, nz, width = val_ref.shape
    rank = width // HEADS

    @pl.when(pl.program_id(0) == 0)
    def _():
        coefficients(lines, pool_ref[...], wqk_ref[...], coef_ref)
        gy, gz = lax.axis_index("gy"), lax.axis_index("gz")
        rows_y = pl.ds(pl.multiple_of(lines[0] + gy * ny, 8), ny)
        rows_z = pl.ds(pl.multiple_of(lines[0] + lines[1] + gz * nz, 8), nz)
        spread_lanes(coef_ref[rows_y, width:], key_y, rank)
        key_z[...] = coef_ref[rows_z, width:].T.astype(BF16)

    mask = head_mask(width, rank)
    for y in range(ny):
        full = dot(key_z[...], val_ref[0, y]).reshape(HEADS, rank, width)
        state[y] = jnp.sum(jnp.where(mask, full, 0.0), axis=0)
    acc = jnp.zeros((rank, rank, width), F32)
    for y in range(ny):
        acc = acc + key_y[y][:, None, :] * state[y][None, :, :]
    out_ref[0] = acc.astype(out_ref.dtype)


def mix_x_kernel(line, coef_ref, in_ref, out_ref, query, key, mid):
    width = in_ref.shape[-1]
    rank = width // HEADS
    spread_lanes(coef_ref[:line, :width], query, rank)
    spread_lanes(coef_ref[:line, width:], key, rank)
    mid[...] = jnp.zeros_like(mid)

    def down(r, carry):
        mid[...] += key[r][:, None, :] * in_ref[r].astype(F32)[None, :, :]
        return carry

    lax.fori_loop(0, line, down, 0)

    def up(p, carry):
        out_ref[p] = jnp.sum(query[p][:, None, :] * mid[...], axis=0).astype(out_ref.dtype)
        return carry

    lax.fori_loop(0, line, up, 0)


def gelu(x):
    return 0.5 * x * (1.0 + jnp.tanh(math.sqrt(2.0 / math.pi) * (x + 0.044715 * (x * x * x))))


def finish_kernel(
    lines, coef_ref, in_ref, tok_ref, wo_ref, wgu_ref, wd_ref, out_ref, query_y, query_z, mixed
):
    _, ny, nz, width = tok_ref.shape
    rank = width // HEADS
    ff = wd_ref.shape[0]

    @pl.when(pl.program_id(0) == 0)
    def _():
        gy, gz = lax.axis_index("gy"), lax.axis_index("gz")
        rows_y = pl.ds(pl.multiple_of(lines[0] + gy * ny, 8), ny)
        rows_z = pl.ds(pl.multiple_of(lines[0] + lines[1] + gz * nz, 8), nz)
        spread_lanes(coef_ref[rows_y, :width], query_y, rank)
        query_z[...] = coef_ref[rows_z, :width].astype(BF16)

    mask = head_mask(width, rank)
    state = in_ref[0].astype(F32)
    avg = averaging(width)
    for y in range(ny):
        line = jnp.sum(query_y[y][:, None, :] * state, axis=0)
        wide = jnp.where(mask, line[None], 0.0).astype(BF16).reshape(HEADS * rank, width)
        mixed[y] = dot(query_z[...], wide).astype(BF16)
    group = 4
    for g in range(0, ny, group):
        rows = group * nz
        tok = tok_ref[0, g : g + group].reshape(rows, width).astype(F32)
        resid = tok + dot(mixed[g : g + group].reshape(rows, width), wo_ref[...])
        cent = resid - jnp.mean(resid, axis=-1, keepdims=True)
        var = dot((cent * cent).astype(BF16), avg)
        inner = (cent * lax.rsqrt(var + EPS)).astype(BF16)
        gate = dot(inner, wgu_ref[:, :ff])
        up = dot(inner, wgu_ref[:, ff:])
        hidden = (gelu(gate) * up).astype(BF16)
        result = resid + dot(hidden, wd_ref[...])
        out_ref[0, g : g + group] = result.astype(BF16).reshape(group, nz, width)


def whole(shape):
    return pl.BlockSpec(shape, lambda i: (0,) * len(shape))


def slab(shape):
    return pl.BlockSpec((1,) + shape[1:], lambda i: (i,) + (0,) * (len(shape) - 1))


def params(**more):
    return pltpu.CompilerParams(vmem_limit_bytes=VMEM_LIMIT, **more)


def body(tokens, w_qkv, w_out, w_gate_up, w_down):
    nx, ny, nz, width = tokens.shape
    rank = width // HEADS
    lines = (nx * lax.axis_size("gx"), ny * lax.axis_size("gy"), nz * lax.axis_size("gz"))
    total = sum(lines)
    w_qk, w_v = w_qkv[:, : 2 * width], w_qkv[:, 2 * width :]

    value, pool = pl.pallas_call(
        functools.partial(project_kernel, lines),
        grid=(nx,),
        in_specs=[slab(tokens.shape), whole(w_v.shape)],
        out_specs=[slab(tokens.shape), whole((total, width))],
        out_shape=[
            jax.ShapeDtypeStruct(tokens.shape, BF16),
            jax.ShapeDtypeStruct((total, width), F32),
        ],
        compiler_params=params(),
        name="project",
    )(tokens, w_v)
    pool = lax.psum(pool, ("gx", "gy", "gz"))

    small = (nx, rank, rank, width)
    state, coef = pl.pallas_call(
        functools.partial(compress_kernel, lines),
        grid=(nx,),
        in_specs=[whole(pool.shape), whole(w_qk.shape), slab(value.shape)],
        out_specs=[slab(small), whole((total, 2 * width))],
        out_shape=[
            jax.ShapeDtypeStruct(small, BF16),
            jax.ShapeDtypeStruct((total, 2 * width), F32),
        ],
        scratch_shapes=[
            pltpu.VMEM((ny, rank, width), F32),
            pltpu.VMEM((width, nz), BF16),
            pltpu.VMEM((ny, rank, width), F32),
        ],
        compiler_params=params(),
        name="compress",
    )(pool, w_qk, value)

    state = lax.psum_scatter(state, ("gy", "gz"), scatter_dimension=1, tiled=True)
    count_x = lax.axis_size("gx")
    part = state.reshape(nx, -1, width)
    part = lax.all_to_all(part, "gx", split_axis=1, concat_axis=0, tiled=True)
    part = pl.pallas_call(
        functools.partial(mix_x_kernel, lines[0]),
        out_shape=jax.ShapeDtypeStruct(part.shape, BF16),
        scratch_shapes=[
            pltpu.VMEM((lines[0], rank, width), F32),
            pltpu.VMEM((lines[0], rank, width), F32),
            pltpu.VMEM((rank,) + part.shape[1:], F32),
        ],
        compiler_params=params(),
        name="mix_x",
    )(coef, part)
    part = lax.all_to_all(part, "gx", split_axis=0, concat_axis=1, tiled=True)
    state = lax.all_gather(part.reshape(state.shape), ("gy", "gz"), axis=1, tiled=True)

    return pl.pallas_call(
        functools.partial(finish_kernel, lines),
        grid=(nx,),
        in_specs=[
            whole(coef.shape),
            slab(small),
            slab(tokens.shape),
            whole(w_out.shape),
            whole(w_gate_up.shape),
            whole(w_down.shape),
        ],
        out_specs=slab(tokens.shape),
        out_shape=jax.ShapeDtypeStruct(tokens.shape, BF16),
        scratch_shapes=[
            pltpu.VMEM((ny, rank, width), F32),
            pltpu.VMEM((nz, width), BF16),
            pltpu.VMEM((ny, nz, width), BF16),
        ],
        compiler_params=params(),
        name="finish",
    )(coef, state, tokens, w_out, w_gate_up, w_down)


def solution(mesh):
    in_specs = (P("gx", "gy", "gz", None), P(), P(), P(), P())
    out_specs = P("gx", "gy", "gz", None)
    return jax.shard_map(body, mesh=mesh, in_specs=in_specs, out_specs=out_specs, check_vma=False)
```

```python
import functools
import math

import jax
import jax.numpy as jnp
from jax import lax
from jax.experimental import pallas as pl
from jax.experimental.pallas import tpu as pltpu
from jax.sharding import PartitionSpec as P

HEADS = 8
EPS = 1e-05
VMEM_LIMIT = 56 * 1024 * 1024
F32 = jnp.float32
BF16 = jnp.bfloat16


def dot(a, b):
    return jnp.dot(a, b, preferred_element_type=F32)


def averaging(width):
    return jnp.full((width, width), 1.0 / width, BF16)


def head_mask(width, rank):
    shape = (HEADS, 1, width)
    lane = lax.broadcasted_iota(jnp.int32, shape, 2)
    return lane // rank == lax.broadcasted_iota(jnp.int32, shape, 0)


def spread_lanes(coef, out_ref, rank):
    width = coef.shape[-1]
    row = lax.broadcasted_iota(jnp.int32, (width, width), 0)
    lane = lax.broadcasted_iota(jnp.int32, (width, width), 1)
    same = row // rank == lane // rank
    for d in range(rank):
        pick = jnp.where(same & (row % rank == d), 1.0, 0.0).astype(BF16)
        out_ref[:, d, :] = dot(coef.astype(BF16), pick)


def coefficients(lines, pool, w_qk, out_ref):
    width = pool.shape[-1]
    rank = width // HEADS
    both = jnp.dot(pool, w_qk.astype(F32), precision=lax.Precision.HIGHEST)
    start = 0
    for length in lines:
        for part in range(2):
            cut = both[start : start + length, part * width : (part + 1) * width]
            total = jnp.sum(jnp.sum(cut * cut, axis=0, keepdims=True), axis=1, keepdims=True)
            unit = cut * lax.rsqrt(total / (length * width) + 1e-06)
            if part == 0:
                unit = unit * (1.0 / math.sqrt(rank * length))
            out_ref[start : start + length, part * width : (part + 1) * width] = unit
        start += length


MESH = pl.DeviceIdType.MESH


def wait_bytes(view, sem):
    pltpu.make_async_copy(view, view, sem).wait()


def attend_kernel(
    sizes,
    lines,
    tok_ref,
    wqkv_ref,
    out_ref,
    coef_ref,
    value,
    pool_x,
    pool_y,
    pool_z,
    give,
    take,
    owned,
    spread,
    pooled,
    key_y,
    key_z,
    state,
    part_out,
    part_in,
    mine,
    x_out,
    x_in,
    query_x,
    key_x,
    mid,
    back_out,
    back_in,
    gathered,
    send,
    recv,
    back_recv,
):
    ci, cj, ck = sizes
    count = ci * cj * ck
    group = cj * ck
    nx, ny, nz, width = tok_ref.shape
    rank = width // HEADS
    gx, gy, gz = (lax.axis_index(a) for a in ("gx", "gy", "gz"))
    me = (gx * cj + gy) * ck + gz
    lane_of = gy * ck + gz

    def place(flat):
        return flat // group, flat // ck % cj, flat % ck

    barrier = pltpu.get_barrier_semaphore()

    def greet(off, carry):
        pl.semaphore_signal(
            barrier, inc=1, device_id=place(lax.rem(me + off, count)), device_id_type=MESH
        )
        return carry

    lax.fori_loop(1, count, greet, 0)

    avg = averaging(width)
    pool_y[...] = jnp.zeros_like(pool_y)
    pool_z[...] = jnp.zeros_like(pool_z)
    give[...] = jnp.zeros_like(give)

    def normalise(x, carry):
        tok = tok_ref[x].reshape(ny * nz, width)
        cent = tok.astype(F32) - dot(tok, avg)
        var = dot((cent * cent).astype(BF16), avg)
        normed = (cent * lax.rsqrt(var + EPS)).astype(BF16)
        value[x] = normed.reshape(ny, nz, width)
        full = normed.astype(F32).reshape(ny, nz, width)
        by_y = jnp.sum(full, axis=1)
        pool_x[pl.ds(x, 1), :] = jnp.sum(by_y, axis=0, keepdims=True)
        pool_y[...] += by_y
        pool_z[...] += jnp.sum(full, axis=0)
        return carry

    lax.fori_loop(0, nx, normalise, 0)

    held_x, held_y, held_z = -(-nx // group), -(-ny // (ci * ck)), -(-nz // (ci * cj))

    def starts(i, j, k):
        return (
            jnp.minimum((j * ck + k) * held_x, nx - held_x),
            jnp.minimum((i * ck + k) * held_y, ny - held_y),
            jnp.minimum((i * cj + j) * held_z, nz - held_z),
        )

    def fill(s, carry):
        at_x, at_y, at_z = starts(*place(s))
        for r in range(held_x):
            give[s, r : r + 1, :] = pool_x[pl.ds(at_x + r, 1), :]
        for r in range(held_y):
            give[s, held_x + r : held_x + r + 1, :] = pool_y[pl.ds(at_y + r, 1), :]
        for r in range(held_z):
            row = held_x + held_y + r
            give[s, row : row + 1, :] = pool_z[pl.ds(at_z + r, 1), :]
        return carry

    lax.fori_loop(0, count, fill, 0)
    pl.semaphore_wait(barrier, count - 1)

    def send_rows(off, carry):
        to = lax.rem(me + off, count)
        pltpu.make_async_remote_copy(
            give.at[to], take.at[me], send.at[0], recv.at[0], device_id=place(to), device_id_type=MESH
        ).start()
        return carry

    lax.fori_loop(1, count, send_rows, 0)
    take[me] = give[me]

    def project(x, carry):
        normed = value[x].reshape(ny * nz, width)
        value[x] = dot(normed, wqkv_ref[:, 2 * width :]).astype(BF16).reshape(ny, nz, width)
        return carry

    lax.fori_loop(0, nx, project, 0)
    wait_bytes(take.at[pl.ds(0, count - 1)], recv.at[0])

    row = lax.broadcasted_iota(jnp.int32, owned.shape, 0)

    def add_rows(s, acc):
        i, j, k = place(s)
        ours = jnp.where(
            row < held_x,
            (i == gx).astype(jnp.int32),
            jnp.where(row < held_x + held_y, (j == gy).astype(jnp.int32), (k == gz).astype(jnp.int32)),
        )
        return acc + jnp.where(ours > 0, take[s], 0.0)

    owned[...] = lax.fori_loop(0, count, add_rows, jnp.zeros(owned.shape, F32))

    def send_owned(off, carry):
        to = lax.rem(me + off, count)
        pltpu.make_async_remote_copy(
            owned, spread.at[me], send.at[1], recv.at[1], device_id=place(to), device_id_type=MESH
        ).start()
        return carry

    lax.fori_loop(1, count, send_owned, 0)
    spread[me] = owned[...]
    wait_bytes(spread.at[pl.ds(0, count - 1)], recv.at[1])

    def unfold(s, carry):
        i, j, k = place(s)
        at_x, at_y, at_z = starts(i, j, k)
        for r in range(held_x):
            pooled[pl.ds(i * nx + at_x + r, 1), :] = spread[s, r : r + 1, :]
        for r in range(held_y):
            pooled[pl.ds(lines[0] + j * ny + at_y + r, 1), :] = spread[s, held_x + r : held_x + r + 1, :]
        for r in range(held_z):
            row = held_x + held_y + r
            pooled[pl.ds(lines[0] + lines[1] + k * nz + at_z + r, 1), :] = spread[s, row : row + 1, :]
        return carry

    lax.fori_loop(0, count, unfold, 0)
    coefficients(lines, pooled[...], wqkv_ref[:, : 2 * width], coef_ref)

    rows_y = pl.ds(pl.multiple_of(lines[0] + gy * ny, 8), ny)
    rows_z = pl.ds(pl.multiple_of(lines[0] + lines[1] + gz * nz, 8), nz)
    spread_lanes(coef_ref[rows_y, width:], key_y, rank)
    key_z[...] = coef_ref[rows_z, width:].T.astype(BF16)
    mask = head_mask(width, rank)
    share = rank // group

    def compress(x, carry):
        for y in range(ny):
            full = dot(key_z[...], value[x, y]).reshape(HEADS, rank, width)
            state[y] = jnp.sum(jnp.where(mask, full, 0.0), axis=0)
        acc = jnp.zeros((rank, rank, width), F32)
        for y in range(ny):
            acc = acc + key_y[y][:, None, :] * state[y][None, :, :]
        part_out[x] = acc.astype(BF16)

        def send_share(off, carry):
            to = lax.rem(lane_of + off, group)
            pltpu.make_async_remote_copy(
                part_out.at[x, pl.ds(to * share, share)],
                part_in.at[lane_of, x],
                send.at[2],
                recv.at[2],
                device_id=(gx, to // ck, to % ck),
                device_id_type=MESH,
            ).start()
            return carry

        lax.fori_loop(1, group, send_share, 0)
        part_in[lane_of, x] = part_out[x, pl.ds(lane_of * share, share)]
        return carry

    lax.fori_loop(0, nx, compress, 0)
    spread_lanes(coef_ref[: lines[0], :width], query_x, rank)
    spread_lanes(coef_ref[: lines[0], width:], key_x, rank)
    wait_bytes(part_in.at[pl.ds(0, group - 1)], recv.at[2])

    rows = share * rank // ci
    total = jnp.zeros((nx, share, rank, width), F32)
    for g in range(group):
        total = total + part_in[g].astype(F32)
    mine[...] = total.reshape(nx, share * rank, width)
    for p in range(ci):
        x_out[p] = mine[:, p * rows : (p + 1) * rows, :].reshape(nx * rows, width).astype(BF16)

    def send_x(off, carry):
        to = lax.rem(gx + off, ci)
        pltpu.make_async_remote_copy(
            x_out.at[to], x_in.at[gx], send.at[3], recv.at[3], device_id=(to, gy, gz), device_id_type=MESH
        ).start()
        return carry

    lax.fori_loop(1, ci, send_x, 0)
    x_in[gx] = x_out[gx]
    wait_bytes(x_in.at[pl.ds(0, ci - 1)], recv.at[3])

    mid[...] = jnp.zeros_like(mid)

    def down(i, carry):
        block = x_in[i].astype(F32).reshape(nx, rows, width)
        acc = mid[...]
        for x in range(nx):
            acc = acc + key_x[i * nx + x][:, None, :] * block[x][None]
        mid[...] = acc
        return carry

    lax.fori_loop(0, ci, down, 0)

    def up(off, carry):
        to = lax.rem(gx + off, ci)
        line = [jnp.sum(query_x[to * nx + x][:, None, :] * mid[...], axis=0) for x in range(nx)]
        back_out[to] = jnp.concatenate(line, axis=0).astype(BF16)
        return carry

    def up_send(off, carry):
        up(off, carry)
        to = lax.rem(gx + off, ci)
        pltpu.make_async_remote_copy(
            back_out.at[to],
            back_in.at[gx],
            send.at[4],
            back_recv.at[gx],
            device_id=(to, gy, gz),
            device_id_type=MESH,
        ).start()
        return carry

    lax.fori_loop(1, ci, up_send, 0)
    up(0, 0)
    back_in[gx] = back_out[gx]

    def forward(chunk):
        def send_chunk(other, carry):
            to = lax.rem(lane_of + other, group)
            pltpu.make_async_remote_copy(
                back_in.at[chunk],
                gathered.at[lane_of, chunk],
                send.at[5],
                recv.at[5],
                device_id=(gx, to // ck, to % ck),
                device_id_type=MESH,
            ).start()
            return carry

        lax.fori_loop(1, group, send_chunk, 0)
        gathered[lane_of, chunk] = back_in[chunk]

    forward(gx)

    def arrive(off, carry):
        chunk = lax.rem(gx + ci - off, ci)
        wait_bytes(back_in.at[chunk], back_recv.at[chunk])
        forward(chunk)
        return carry

    lax.fori_loop(1, ci, arrive, 0)
    wait_bytes(gathered.at[pl.ds(0, group - 1)], recv.at[5])
    for g in range(group):
        for q in range(ci):
            at = (g * ci + q) * rows
            out_ref[:, at : at + rows, :] = gathered[g, q].astype(F32).reshape(nx, rows, width)

    wait_bytes(give.at[pl.ds(0, count - 1)], send.at[0])
    wait_bytes(spread.at[pl.ds(0, count - 1)], send.at[1])
    wait_bytes(part_in.at[pl.ds(0, group - 1)], send.at[2])
    wait_bytes(x_out.at[pl.ds(0, ci - 1)], send.at[3])
    wait_bytes(back_out.at[pl.ds(0, ci - 1)], send.at[4])
    wait_bytes(gathered.at[pl.ds(0, group - 1)], send.at[5])


def gelu(x):
    return 0.5 * x * (1.0 + jnp.tanh(math.sqrt(2.0 / math.pi) * (x + 0.044715 * (x * x * x))))


def finish_kernel(
    lines, coef_ref, in_ref, tok_ref, wo_ref, wgu_ref, wd_ref, out_ref, query_y, query_z, mixed
):
    _, ny, nz, width = tok_ref.shape
    rank = width // HEADS
    ff = wd_ref.shape[0]

    @pl.when(pl.program_id(0) == 0)
    def _():
        gy, gz = lax.axis_index("gy"), lax.axis_index("gz")
        rows_y = pl.ds(pl.multiple_of(lines[0] + gy * ny, 8), ny)
        rows_z = pl.ds(pl.multiple_of(lines[0] + lines[1] + gz * nz, 8), nz)
        spread_lanes(coef_ref[rows_y, :width], query_y, rank)
        query_z[...] = coef_ref[rows_z, :width].astype(BF16)

    mask = head_mask(width, rank)
    state = in_ref[0].reshape(rank, rank, width)
    avg = averaging(width)
    for y in range(ny):
        line = jnp.sum(query_y[y][:, None, :] * state, axis=0)
        wide = jnp.where(mask, line[None], 0.0).astype(BF16).reshape(HEADS * rank, width)
        mixed[y] = dot(query_z[...], wide).astype(BF16)
    group = 4
    for g in range(0, ny, group):
        rows = group * nz
        tok = tok_ref[0, g : g + group].reshape(rows, width).astype(F32)
        resid = tok + dot(mixed[g : g + group].reshape(rows, width), wo_ref[...])
        cent = resid - jnp.mean(resid, axis=-1, keepdims=True)
        var = dot((cent * cent).astype(BF16), avg)
        inner = (cent * lax.rsqrt(var + EPS)).astype(BF16)
        gate = dot(inner, wgu_ref[:, :ff])
        up = dot(inner, wgu_ref[:, ff:])
        hidden = (gelu(gate) * up).astype(BF16)
        result = resid + dot(hidden, wd_ref[...])
        out_ref[0, g : g + group] = result.astype(BF16).reshape(group, nz, width)


def whole(shape):
    return pl.BlockSpec(shape, lambda i: (0,) * len(shape))


def slab(shape):
    return pl.BlockSpec((1,) + shape[1:], lambda i: (i,) + (0,) * (len(shape) - 1))


def params(**more):
    return pltpu.CompilerParams(vmem_limit_bytes=VMEM_LIMIT, **more)


def body(tokens, w_qkv, w_out, w_gate_up, w_down):
    nx, ny, nz, width = tokens.shape
    rank = width // HEADS
    lines = (nx * lax.axis_size("gx"), ny * lax.axis_size("gy"), nz * lax.axis_size("gz"))
    total = sum(lines)
    sizes = tuple(lax.axis_size(a) for a in ("gx", "gy", "gz"))
    count, group = math.prod(sizes), sizes[1] * sizes[2]
    held = -(-nx // group) - (-ny // (sizes[0] * sizes[2])) - (-nz // (sizes[0] * sizes[1]))
    held = -(-held // 8) * 8
    share = rank // group
    rows = share * rank // sizes[0]
    small = (nx, rank * rank, width)
    state, coef = pl.pallas_call(
        functools.partial(attend_kernel, sizes, lines),
        in_specs=[pl.BlockSpec(memory_space=pltpu.VMEM)] * 2,
        out_specs=[pl.BlockSpec(memory_space=pltpu.VMEM)] * 2,
        out_shape=[
            jax.ShapeDtypeStruct(small, F32),
            jax.ShapeDtypeStruct((total, 2 * width), F32),
        ],
        scratch_shapes=[
            pltpu.VMEM(tokens.shape, BF16),
            pltpu.VMEM((nx, width), F32),
            pltpu.VMEM((ny, width), F32),
            pltpu.VMEM((nz, width), F32),
            pltpu.VMEM((count, held, width), F32),
            pltpu.VMEM((count, held, width), F32),
            pltpu.VMEM((held, width), F32),
            pltpu.VMEM((count, held, width), F32),
            pltpu.VMEM((total, width), F32),
            pltpu.VMEM((ny, rank, width), F32),
            pltpu.VMEM((width, nz), BF16),
            pltpu.VMEM((ny, rank, width), F32),
            pltpu.VMEM((nx, rank, rank, width), BF16),
            pltpu.VMEM((group, nx, share, rank, width), BF16),
            pltpu.VMEM((nx, share * rank, width), F32),
            pltpu.VMEM((sizes[0], nx * rows, width), BF16),
            pltpu.VMEM((sizes[0], nx * rows, width), BF16),
            pltpu.VMEM((lines[0], rank, width), F32),
            pltpu.VMEM((lines[0], rank, width), F32),
            pltpu.VMEM((rank, rows, width), F32),
            pltpu.VMEM((sizes[0], nx * rows, width), BF16),
            pltpu.VMEM((sizes[0], nx * rows, width), BF16),
            pltpu.VMEM((group, sizes[0], nx * rows, width), BF16),
            pltpu.SemaphoreType.DMA((6,)),
            pltpu.SemaphoreType.DMA((6,)),
            pltpu.SemaphoreType.DMA((sizes[0],)),
        ],
        compiler_params=params(collective_id=0, has_side_effects=True),
        name="attend",
    )(tokens, w_qkv)

    return pl.pallas_call(
        functools.partial(finish_kernel, lines),
        grid=(nx,),
        in_specs=[
            whole(coef.shape),
            slab(small),
            slab(tokens.shape),
            whole(w_out.shape),
            whole(w_gate_up.shape),
            whole(w_down.shape),
        ],
        out_specs=slab(tokens.shape),
        out_shape=jax.ShapeDtypeStruct(tokens.shape, BF16),
        scratch_shapes=[
            pltpu.VMEM((ny, rank, width), F32),
            pltpu.VMEM((nz, width), BF16),
            pltpu.VMEM((ny, nz, width), BF16),
        ],
        compiler_params=params(),
        name="finish",
    )(coef, state, tokens, w_out, w_gate_up, w_down)


def solution(mesh):
    in_specs = (P("gx", "gy", "gz", None), P(), P(), P(), P())
    out_specs = P("gx", "gy", "gz", None)
    return jax.shard_map(body, mesh=mesh, in_specs=in_specs, out_specs=out_specs, check_vma=False)
```

```python
import functools
import math

import jax
import jax.numpy as jnp
from jax import lax
from jax.experimental import pallas as pl
from jax.experimental.pallas import tpu as pltpu
from jax.sharding import PartitionSpec as P

HEADS = 8
EPS = 1e-05
VMEM_LIMIT = 56 * 1024 * 1024
F32 = jnp.float32
BF16 = jnp.bfloat16


def dot(a, b):
    return jnp.dot(a, b, preferred_element_type=F32)


def averaging(width):
    return jnp.full((width, width), 1.0 / width, BF16)


def head_mask(width, rank):
    shape = (HEADS, 1, width)
    lane = lax.broadcasted_iota(jnp.int32, shape, 2)
    return lane // rank == lax.broadcasted_iota(jnp.int32, shape, 0)


def spread_lanes(coef, out_ref, rank):
    width = coef.shape[-1]
    row = lax.broadcasted_iota(jnp.int32, (width, width), 0)
    lane = lax.broadcasted_iota(jnp.int32, (width, width), 1)
    same = row // rank == lane // rank
    for d in range(rank):
        pick = jnp.where(same & (row % rank == d), 1.0, 0.0).astype(BF16)
        out_ref[d] = dot(coef.astype(BF16), pick)


def coefficients(lines, pool, w_qk, out_ref):
    width = pool.shape[-1]
    rank = width // HEADS
    both = jnp.dot(pool, w_qk.astype(F32), precision=lax.Precision.HIGHEST)
    start = 0
    for length in lines:
        for part in range(2):
            cut = both[start : start + length, part * width : (part + 1) * width]
            total = jnp.sum(jnp.sum(cut * cut, axis=0, keepdims=True), axis=1, keepdims=True)
            unit = cut * lax.rsqrt(total / (length * width) + 1e-06)
            if part == 0:
                unit = unit * (1.0 / math.sqrt(rank * length))
            out_ref[start : start + length, part * width : (part + 1) * width] = unit
        start += length


MESH = pl.DeviceIdType.MESH


def wait_bytes(view, sem):
    pltpu.make_async_copy(view, view, sem).wait()


def attend_kernel(
    sizes,
    lines,
    tok_ref,
    wqkv_ref,
    out_ref,
    coef_ref,
    value,
    pool_x,
    pool_y,
    pool_z,
    give,
    take,
    owned,
    spread,
    pooled,
    key_y,
    key_z,
    state,
    part_out,
    part_in,
    mine,
    x_out,
    x_in,
    query_x,
    key_x,
    mid,
    back_out,
    back_in,
    gathered,
    send,
    recv,
    back_recv,
):
    ci, cj, ck = sizes
    count = ci * cj * ck
    group = cj * ck
    nx, ny, nz, width = tok_ref.shape
    rank = width // HEADS
    gx, gy, gz = (lax.axis_index(a) for a in ("gx", "gy", "gz"))
    me = (gx * cj + gy) * ck + gz
    lane_of = gy * ck + gz

    def place(flat):
        return flat // group, flat // ck % cj, flat % ck

    barrier = pltpu.get_barrier_semaphore()

    def greet(off, carry):
        pl.semaphore_signal(
            barrier, inc=1, device_id=place(lax.rem(me + off, count)), device_id_type=MESH
        )
        return carry

    lax.fori_loop(1, count, greet, 0)

    avg = averaging(width)
    pool_y[...] = jnp.zeros_like(pool_y)
    pool_z[...] = jnp.zeros_like(pool_z)
    give[...] = jnp.zeros_like(give)

    def normalise(x, carry):
        tok = tok_ref[x].reshape(ny * nz, width)
        cent = tok.astype(F32) - dot(tok, avg)
        var = dot((cent * cent).astype(BF16), avg)
        normed = (cent * lax.rsqrt(var + EPS)).astype(BF16)
        value[x] = normed.reshape(ny, nz, width)
        full = normed.astype(F32).reshape(ny, nz, width)
        by_y = jnp.sum(full, axis=1)
        pool_x[pl.ds(x, 1), :] = jnp.sum(by_y, axis=0, keepdims=True)
        pool_y[...] += by_y
        pool_z[...] += jnp.sum(full, axis=0)
        return carry

    lax.fori_loop(0, nx, normalise, 0)

    held_x, held_y, held_z = -(-nx // group), -(-ny // (ci * ck)), -(-nz // (ci * cj))

    def starts(i, j, k):
        return (
            jnp.minimum((j * ck + k) * held_x, nx - held_x),
            jnp.minimum((i * ck + k) * held_y, ny - held_y),
            jnp.minimum((i * cj + j) * held_z, nz - held_z),
        )

    def fill(s, carry):
        at_x, at_y, at_z = starts(*place(s))
        for r in range(held_x):
            give[s, r : r + 1, :] = pool_x[pl.ds(at_x + r, 1), :]
        for r in range(held_y):
            give[s, held_x + r : held_x + r + 1, :] = pool_y[pl.ds(at_y + r, 1), :]
        for r in range(held_z):
            row = held_x + held_y + r
            give[s, row : row + 1, :] = pool_z[pl.ds(at_z + r, 1), :]
        return carry

    lax.fori_loop(0, count, fill, 0)
    pl.semaphore_wait(barrier, count - 1)

    def send_rows(off, carry):
        to = lax.rem(me + off, count)
        pltpu.make_async_remote_copy(
            give.at[to], take.at[me], send.at[0], recv.at[0], device_id=place(to), device_id_type=MESH
        ).start()
        return carry

    lax.fori_loop(1, count, send_rows, 0)
    take[me] = give[me]

    def project(x, carry):
        normed = value[x].reshape(ny * nz, width)
        value[x] = dot(normed, wqkv_ref[:, 2 * width :]).astype(BF16).reshape(ny, nz, width)
        return carry

    lax.fori_loop(0, nx, project, 0)
    wait_bytes(take.at[pl.ds(0, count - 1)], recv.at[0])

    row = lax.broadcasted_iota(jnp.int32, owned.shape, 0)

    def add_rows(s, acc):
        i, j, k = place(s)
        ours = jnp.where(
            row < held_x,
            (i == gx).astype(jnp.int32),
            jnp.where(row < held_x + held_y, (j == gy).astype(jnp.int32), (k == gz).astype(jnp.int32)),
        )
        return acc + jnp.where(ours > 0, take[s], 0.0)

    owned[...] = lax.fori_loop(0, count, add_rows, jnp.zeros(owned.shape, F32))

    def send_owned(off, carry):
        to = lax.rem(me + off, count)
        pltpu.make_async_remote_copy(
            owned, spread.at[me], send.at[1], recv.at[1], device_id=place(to), device_id_type=MESH
        ).start()
        return carry

    lax.fori_loop(1, count, send_owned, 0)
    spread[me] = owned[...]
    wait_bytes(spread.at[pl.ds(0, count - 1)], recv.at[1])

    def unfold(s, carry):
        i, j, k = place(s)
        at_x, at_y, at_z = starts(i, j, k)
        for r in range(held_x):
            pooled[pl.ds(i * nx + at_x + r, 1), :] = spread[s, r : r + 1, :]
        for r in range(held_y):
            pooled[pl.ds(lines[0] + j * ny + at_y + r, 1), :] = spread[s, held_x + r : held_x + r + 1, :]
        for r in range(held_z):
            row = held_x + held_y + r
            pooled[pl.ds(lines[0] + lines[1] + k * nz + at_z + r, 1), :] = spread[s, row : row + 1, :]
        return carry

    lax.fori_loop(0, count, unfold, 0)
    coefficients(lines, pooled[...], wqkv_ref[:, : 2 * width], coef_ref)

    rows_y = pl.ds(pl.multiple_of(lines[0] + gy * ny, 8), ny)
    rows_z = pl.ds(pl.multiple_of(lines[0] + lines[1] + gz * nz, 8), nz)
    spread_lanes(coef_ref[rows_y, width:], key_y, rank)
    key_z[...] = coef_ref[rows_z, width:].T.astype(BF16)
    mask = head_mask(width, rank)
    share = rank // group

    def compress(x, carry):
        for y in range(0, ny, 2):
            pair = dot(key_z[...], jnp.concatenate([value[x, y], value[x, y + 1]], axis=1))
            for e in range(2):
                full = pair[:, e * width : (e + 1) * width].reshape(HEADS, rank, width)
                state[y + e] = jnp.sum(jnp.where(mask, full, 0.0), axis=0)
        acc = jnp.zeros((rank, rank, width), F32)
        for y in range(ny):
            acc = acc + key_y[:, y : y + 1, :] * state[y][None, :, :]
        part_out[x] = acc.astype(BF16)

        def send_share(off, carry):
            to = lax.rem(lane_of + off, group)
            pltpu.make_async_remote_copy(
                part_out.at[x, pl.ds(to * share, share)],
                part_in.at[lane_of, x],
                send.at[2],
                recv.at[2],
                device_id=(gx, to // ck, to % ck),
                device_id_type=MESH,
            ).start()
            return carry

        lax.fori_loop(1, group, send_share, 0)
        part_in[lane_of, x] = part_out[x, pl.ds(lane_of * share, share)]
        return carry

    lax.fori_loop(0, nx, compress, 0)
    spread_lanes(coef_ref[: lines[0], :width], query_x, rank)
    spread_lanes(coef_ref[: lines[0], width:], key_x, rank)
    wait_bytes(part_in.at[pl.ds(0, group - 1)], recv.at[2])

    rows = share * rank // ci
    total = jnp.zeros((nx, share, rank, width), F32)
    for g in range(group):
        total = total + part_in[g].astype(F32)
    mine[...] = total.reshape(nx, share * rank, width)
    for p in range(ci):
        x_out[p] = mine[:, p * rows : (p + 1) * rows, :].reshape(nx * rows, width).astype(BF16)

    def send_x(off, carry):
        to = lax.rem(gx + off, ci)
        pltpu.make_async_remote_copy(
            x_out.at[to], x_in.at[gx], send.at[3], recv.at[3], device_id=(to, gy, gz), device_id_type=MESH
        ).start()
        return carry

    lax.fori_loop(1, ci, send_x, 0)
    x_in[gx] = x_out[gx]
    wait_bytes(x_in.at[pl.ds(0, ci - 1)], recv.at[3])

    mid[...] = jnp.zeros_like(mid)

    def down(i, carry):
        block = x_in[i].astype(F32).reshape(nx, rows, width)
        acc = mid[...]
        for x in range(nx):
            acc = acc + key_x[:, pl.ds(i * nx + x, 1), :] * block[x][None]
        mid[...] = acc
        return carry

    lax.fori_loop(0, ci, down, 0)

    def up(off, carry):
        to = lax.rem(gx + off, ci)
        line = [jnp.sum(query_x[:, pl.ds(to * nx + x, 1), :] * mid[...], axis=0) for x in range(nx)]
        back_out[to] = jnp.concatenate(line, axis=0).astype(BF16)
        return carry

    def up_send(off, carry):
        up(off, carry)
        to = lax.rem(gx + off, ci)
        pltpu.make_async_remote_copy(
            back_out.at[to],
            back_in.at[gx],
            send.at[4],
            back_recv.at[gx],
            device_id=(to, gy, gz),
            device_id_type=MESH,
        ).start()
        return carry

    lax.fori_loop(1, ci, up_send, 0)
    up(0, 0)
    back_in[gx] = back_out[gx]

    def forward(chunk):
        def send_chunk(other, carry):
            to = lax.rem(lane_of + other, group)
            pltpu.make_async_remote_copy(
                back_in.at[chunk],
                gathered.at[lane_of, chunk],
                send.at[5],
                recv.at[5],
                device_id=(gx, to // ck, to % ck),
                device_id_type=MESH,
            ).start()
            return carry

        lax.fori_loop(1, group, send_chunk, 0)
        gathered[lane_of, chunk] = back_in[chunk]

    forward(gx)

    def arrive(off, carry):
        chunk = lax.rem(gx + ci - off, ci)
        wait_bytes(back_in.at[chunk], back_recv.at[chunk])
        forward(chunk)
        return carry

    lax.fori_loop(1, ci, arrive, 0)
    wait_bytes(gathered.at[pl.ds(0, group - 1)], recv.at[5])
    for g in range(group):
        for q in range(ci):
            at = (g * ci + q) * rows
            out_ref[:, at : at + rows, :] = gathered[g, q].astype(F32).reshape(nx, rows, width)

    wait_bytes(give.at[pl.ds(0, count - 1)], send.at[0])
    wait_bytes(spread.at[pl.ds(0, count - 1)], send.at[1])
    wait_bytes(part_in.at[pl.ds(0, group - 1)], send.at[2])
    wait_bytes(x_out.at[pl.ds(0, ci - 1)], send.at[3])
    wait_bytes(back_out.at[pl.ds(0, ci - 1)], send.at[4])
    wait_bytes(gathered.at[pl.ds(0, group - 1)], send.at[5])


def twice_gelu_times(x, up):
    scale = math.sqrt(2.0 / math.pi)
    tanh = jnp.tanh(x * (x * x * jnp.array(scale * 0.044715, x.dtype) + jnp.array(scale, x.dtype)))
    both = x * up
    return both * tanh + both


def finish_kernel(
    lines, coef_ref, in_ref, tok_ref, wo_ref, wgu_ref, wd_ref, out_ref, query_y, query_z, mixed
):
    _, ny, nz, width = tok_ref.shape
    rank = width // HEADS
    ff = wd_ref.shape[0]

    @pl.when(pl.program_id(0) == 0)
    def _():
        gy, gz = lax.axis_index("gy"), lax.axis_index("gz")
        rows_y = pl.ds(pl.multiple_of(lines[0] + gy * ny, 8), ny)
        rows_z = pl.ds(pl.multiple_of(lines[0] + lines[1] + gz * nz, 8), nz)
        spread_lanes(coef_ref[rows_y, :width], query_y, rank)
        query_z[...] = coef_ref[rows_z, :width].astype(BF16)

    mask = jnp.broadcast_to(jnp.where(head_mask(width, rank), 1.0, 0.0), (HEADS, rank, width)).astype(BF16)
    state = in_ref[0].reshape(rank, rank, width)
    avg = averaging(width)
    for y in range(0, ny, 2):
        wide = []
        for e in range(2):
            line = jnp.sum(query_y[:, y + e : y + e + 1, :] * state, axis=0).astype(BF16)
            wide.append((mask * line[None]).reshape(HEADS * rank, width))
        pair = dot(query_z[...], jnp.concatenate(wide, axis=1)).astype(BF16)
        mixed[y] = pair[:, :width]
        mixed[y + 1] = pair[:, width:]
    group = 4
    for g in range(0, ny, group):
        rows = group * nz
        tok = tok_ref[0, g : g + group].reshape(rows, width).astype(F32)
        resid = tok + dot(mixed[g : g + group].reshape(rows, width), wo_ref[...])
        high = resid.astype(BF16)
        low = (resid - high.astype(F32)).astype(BF16)
        cent = resid - (dot(high, avg) + dot(low, avg))
        var = dot((cent * cent).astype(BF16), avg)
        inner = (cent * lax.rsqrt(var + EPS)).astype(BF16)
        gate = dot(inner, wgu_ref[:, :ff]).astype(BF16)
        up = dot(inner, wgu_ref[:, ff:]).astype(BF16)
        result = resid + 0.5 * dot(twice_gelu_times(gate, up), wd_ref[...])
        out_ref[0, g : g + group] = result.astype(BF16).reshape(group, nz, width)


def whole(shape):
    return pl.BlockSpec(shape, lambda i: (0,) * len(shape))


def slab(shape):
    return pl.BlockSpec((1,) + shape[1:], lambda i: (i,) + (0,) * (len(shape) - 1))


def params(**more):
    return pltpu.CompilerParams(vmem_limit_bytes=VMEM_LIMIT, **more)


def body(tokens, w_qkv, w_out, w_gate_up, w_down):
    nx, ny, nz, width = tokens.shape
    rank = width // HEADS
    lines = (nx * lax.axis_size("gx"), ny * lax.axis_size("gy"), nz * lax.axis_size("gz"))
    total = sum(lines)
    sizes = tuple(lax.axis_size(a) for a in ("gx", "gy", "gz"))
    count, group = math.prod(sizes), sizes[1] * sizes[2]
    held = -(-nx // group) - (-ny // (sizes[0] * sizes[2])) - (-nz // (sizes[0] * sizes[1]))
    held = -(-held // 8) * 8
    share = rank // group
    rows = share * rank // sizes[0]
    small = (nx, rank * rank, width)
    state, coef = pl.pallas_call(
        functools.partial(attend_kernel, sizes, lines),
        in_specs=[pl.BlockSpec(memory_space=pltpu.VMEM)] * 2,
        out_specs=[pl.BlockSpec(memory_space=pltpu.VMEM)] * 2,
        out_shape=[
            jax.ShapeDtypeStruct(small, F32),
            jax.ShapeDtypeStruct((total, 2 * width), F32),
        ],
        scratch_shapes=[
            pltpu.VMEM(tokens.shape, BF16),
            pltpu.VMEM((nx, width), F32),
            pltpu.VMEM((ny, width), F32),
            pltpu.VMEM((nz, width), F32),
            pltpu.VMEM((count, held, width), F32),
            pltpu.VMEM((count, held, width), F32),
            pltpu.VMEM((held, width), F32),
            pltpu.VMEM((count, held, width), F32),
            pltpu.VMEM((total, width), F32),
            pltpu.VMEM((rank, ny, width), F32),
            pltpu.VMEM((width, nz), BF16),
            pltpu.VMEM((ny, rank, width), F32),
            pltpu.VMEM((nx, rank, rank, width), BF16),
            pltpu.VMEM((group, nx, share, rank, width), BF16),
            pltpu.VMEM((nx, share * rank, width), F32),
            pltpu.VMEM((sizes[0], nx * rows, width), BF16),
            pltpu.VMEM((sizes[0], nx * rows, width), BF16),
            pltpu.VMEM((rank, lines[0], width), F32),
            pltpu.VMEM((rank, lines[0], width), F32),
            pltpu.VMEM((rank, rows, width), F32),
            pltpu.VMEM((sizes[0], nx * rows, width), BF16),
            pltpu.VMEM((sizes[0], nx * rows, width), BF16),
            pltpu.VMEM((group, sizes[0], nx * rows, width), BF16),
            pltpu.SemaphoreType.DMA((6,)),
            pltpu.SemaphoreType.DMA((6,)),
            pltpu.SemaphoreType.DMA((sizes[0],)),
        ],
        compiler_params=params(collective_id=0, has_side_effects=True),
        name="attend",
    )(tokens, w_qkv)

    return pl.pallas_call(
        functools.partial(finish_kernel, lines),
        grid=(nx,),
        in_specs=[
            whole(coef.shape),
            slab(small),
            slab(tokens.shape),
            whole(w_out.shape),
            whole(w_gate_up.shape),
            whole(w_down.shape),
        ],
        out_specs=slab(tokens.shape),
        out_shape=jax.ShapeDtypeStruct(tokens.shape, BF16),
        scratch_shapes=[
            pltpu.VMEM((rank, ny, width), F32),
            pltpu.VMEM((nz, width), BF16),
            pltpu.VMEM((ny, nz, width), BF16),
        ],
        compiler_params=params(),
        name="finish",
    )(coef, state, tokens, w_out, w_gate_up, w_down)


def solution(mesh):
    in_specs = (P("gx", "gy", "gz", None), P(), P(), P(), P())
    out_specs = P("gx", "gy", "gz", None)
    return jax.shard_map(body, mesh=mesh, in_specs=in_specs, out_specs=out_specs, check_vma=False)
```

```python
import functools
import math

import jax
import jax.numpy as jnp
from jax import lax
from jax.experimental import pallas as pl
from jax.experimental.pallas import tpu as pltpu
from jax.sharding import PartitionSpec as P

HEADS = 8
EPS = 1e-05
VMEM_LIMIT = 56 * 1024 * 1024
F32 = jnp.float32
BF16 = jnp.bfloat16


def dot(a, b):
    return jnp.dot(a, b, preferred_element_type=F32)


def averaging(width):
    return jnp.full((width, width), 1.0 / width, BF16)


def head_mask(width, rank):
    shape = (HEADS, 1, width)
    lane = lax.broadcasted_iota(jnp.int32, shape, 2)
    return lane // rank == lax.broadcasted_iota(jnp.int32, shape, 0)


def spread_lanes(coef, out_ref, rank):
    width = coef.shape[-1]
    row = lax.broadcasted_iota(jnp.int32, (width, width), 0)
    lane = lax.broadcasted_iota(jnp.int32, (width, width), 1)
    same = row // rank == lane // rank
    for d in range(rank):
        pick = jnp.where(same & (row % rank == d), 1.0, 0.0).astype(BF16)
        out_ref[d] = dot(coef.astype(BF16), pick)


def coefficients(lines, pool, w_qk, out_ref):
    width = pool.shape[-1]
    rank = width // HEADS
    both = jnp.dot(pool, w_qk.astype(F32), precision=lax.Precision.HIGHEST)
    start = 0
    for length in lines:
        for part in range(2):
            cut = both[start : start + length, part * width : (part + 1) * width]
            total = jnp.sum(jnp.sum(cut * cut, axis=0, keepdims=True), axis=1, keepdims=True)
            unit = cut * lax.rsqrt(total / (length * width) + 1e-06)
            if part == 0:
                unit = unit * (1.0 / math.sqrt(rank * length))
            out_ref[start : start + length, part * width : (part + 1) * width] = unit
        start += length


MESH = pl.DeviceIdType.MESH


def wait_bytes(view, sem):
    pltpu.make_async_copy(view, view, sem).wait()


def attend_kernel(
    sizes,
    lines,
    tok_ref,
    wqkv_ref,
    out_ref,
    coef_ref,
    value,
    pool_x,
    pool_y,
    pool_z,
    give,
    take,
    owned,
    spread,
    pooled,
    key_y,
    key_z,
    state,
    part_out,
    part_in,
    mine,
    x_out,
    x_in,
    query_x,
    key_x,
    mid,
    back_out,
    back_in,
    gathered,
    send,
    recv,
    back_recv,
    cross_recv,
):
    ci, cj, ck = sizes
    count = ci * cj * ck
    group = cj * ck
    nx, ny, nz, width = tok_ref.shape
    rank = width // HEADS
    gx, gy, gz = (lax.axis_index(a) for a in ("gx", "gy", "gz"))
    me = (gx * cj + gy) * ck + gz
    lane_of = gy * ck + gz

    def place(flat):
        return lax.div(flat, group), lax.rem(lax.div(flat, ck), cj), lax.rem(flat, ck)

    barrier = pltpu.get_barrier_semaphore()

    def greet(off, carry):
        pl.semaphore_signal(
            barrier, inc=1, device_id=place(lax.rem(me + off, count)), device_id_type=MESH
        )
        return carry

    lax.fori_loop(1, count, greet, 0)

    avg = averaging(width)
    pool_y[...] = jnp.zeros_like(pool_y)
    pool_z[...] = jnp.zeros_like(pool_z)
    give[...] = jnp.zeros_like(give)

    piece = 4

    def normalise(x, carry):
        by_y, by_z = [], jnp.zeros((nz, width), F32)
        for y in range(0, ny, piece):
            tok = tok_ref[x, y : y + piece].reshape(piece * nz, width)
            cent = tok.astype(F32) - dot(tok, avg)
            var = dot((cent * cent).astype(BF16), avg)
            normed = (cent * lax.rsqrt(var + EPS)).astype(BF16)
            value[x, y : y + piece] = normed.reshape(piece, nz, width)
            full = normed.astype(F32).reshape(piece, nz, width)
            by_y.append(jnp.sum(full, axis=1))
            by_z = by_z + jnp.sum(full, axis=0)
        by_y = jnp.concatenate(by_y, axis=0)
        pool_x[pl.ds(x, 1), :] = jnp.sum(by_y, axis=0, keepdims=True)
        pool_y[...] += by_y
        pool_z[...] += by_z
        return carry

    lax.fori_loop(0, nx, normalise, 0)

    held_x, held_y, held_z = -(-nx // group), -(-ny // (ci * ck)), -(-nz // (ci * cj))

    def starts(i, j, k):
        return (
            jnp.minimum((j * ck + k) * held_x, nx - held_x),
            jnp.minimum((i * ck + k) * held_y, ny - held_y),
            jnp.minimum((i * cj + j) * held_z, nz - held_z),
        )

    def fill(s, carry):
        at_x, at_y, at_z = starts(*place(s))
        for r in range(held_x):
            give[s, r : r + 1, :] = pool_x[pl.ds(at_x + r, 1), :]
        for r in range(held_y):
            give[s, held_x + r : held_x + r + 1, :] = pool_y[pl.ds(at_y + r, 1), :]
        for r in range(held_z):
            row = held_x + held_y + r
            give[s, row : row + 1, :] = pool_z[pl.ds(at_z + r, 1), :]
        return carry

    lax.fori_loop(0, count, fill, 0, unroll=4)
    pl.semaphore_wait(barrier, count - 1)

    def send_rows(off, carry):
        to = lax.rem(me + off, count)
        pltpu.make_async_remote_copy(
            give.at[to], take.at[me], send.at[0], recv.at[0], device_id=place(to), device_id_type=MESH
        ).start()
        return carry

    lax.fori_loop(1, count, send_rows, 0, unroll=4)
    take[me] = give[me]

    def project(x, carry):
        normed = value[x].reshape(ny * nz, width)
        value[x] = dot(normed, wqkv_ref[:, 2 * width :]).astype(BF16).reshape(ny, nz, width)
        return carry

    lax.fori_loop(0, nx, project, 0)
    wait_bytes(take.at[pl.ds(0, count - 1)], recv.at[0])

    row = lax.broadcasted_iota(jnp.int32, owned.shape, 0)

    def add_rows(s, acc):
        i, j, k = place(s)
        ours = jnp.where(
            row < held_x,
            (i == gx).astype(jnp.int32),
            jnp.where(row < held_x + held_y, (j == gy).astype(jnp.int32), (k == gz).astype(jnp.int32)),
        )
        return acc + jnp.where(ours > 0, take[s], 0.0)

    owned[...] = lax.fori_loop(0, count, add_rows, jnp.zeros(owned.shape, F32), unroll=4)

    def send_owned(off, carry):
        to = lax.rem(me + off, count)
        pltpu.make_async_remote_copy(
            owned, spread.at[me], send.at[1], recv.at[1], device_id=place(to), device_id_type=MESH
        ).start()
        return carry

    lax.fori_loop(1, count, send_owned, 0, unroll=4)
    spread[me] = owned[...]
    wait_bytes(spread.at[pl.ds(0, count - 1)], recv.at[1])

    def unfold(s, carry):
        i, j, k = place(s)
        at_x, at_y, at_z = starts(i, j, k)
        for r in range(held_x):
            pooled[pl.ds(i * nx + at_x + r, 1), :] = spread[s, r : r + 1, :]
        for r in range(held_y):
            pooled[pl.ds(lines[0] + j * ny + at_y + r, 1), :] = spread[s, held_x + r : held_x + r + 1, :]
        for r in range(held_z):
            row = held_x + held_y + r
            pooled[pl.ds(lines[0] + lines[1] + k * nz + at_z + r, 1), :] = spread[s, row : row + 1, :]
        return carry

    lax.fori_loop(0, count, unfold, 0, unroll=4)
    coefficients(lines, pooled[...], wqkv_ref[:, : 2 * width], coef_ref)

    rows_y = pl.ds(pl.multiple_of(lines[0] + gy * ny, 8), ny)
    rows_z = pl.ds(pl.multiple_of(lines[0] + lines[1] + gz * nz, 8), nz)
    spread_lanes(coef_ref[rows_y, width:], key_y, rank)
    key_z[...] = coef_ref[rows_z, width:].T.astype(BF16)
    mask = head_mask(width, rank)
    share = rank // group

    def compress(x, carry):
        for y in range(0, ny, 2):
            pair = dot(key_z[...], jnp.concatenate([value[x, y], value[x, y + 1]], axis=1))
            for e in range(2):
                full = pair[:, e * width : (e + 1) * width].reshape(HEADS, rank, width)
                state[y + e] = jnp.sum(jnp.where(mask, full, 0.0), axis=0)
        acc = jnp.zeros((rank, rank, width), F32)
        for y in range(ny):
            acc = acc + key_y[:, y : y + 1, :] * state[y][None, :, :]
        part_out[x] = acc.astype(BF16)

        def send_share(off, carry):
            to = lax.rem(lane_of + off, group)
            pltpu.make_async_remote_copy(
                part_out.at[x, pl.ds(to * share, share)],
                part_in.at[lane_of, x],
                send.at[2],
                recv.at[2],
                device_id=(gx, to // ck, to % ck),
                device_id_type=MESH,
            ).start()
            return carry

        lax.fori_loop(1, group, send_share, 0)
        part_in[lane_of, x] = part_out[x, pl.ds(lane_of * share, share)]
        return carry

    lax.fori_loop(0, nx, compress, 0)
    spread_lanes(coef_ref[: lines[0], :width], query_x, rank)
    spread_lanes(coef_ref[: lines[0], width:], key_x, rank)
    wait_bytes(part_in.at[pl.ds(0, group - 1)], recv.at[2])

    rows = share * rank // ci
    total = jnp.zeros((nx, share, rank, width), F32)
    for g in range(group):
        total = total + part_in[g].astype(F32)
    mine[...] = total.reshape(nx, share * rank, width)
    for p in range(ci):
        x_out[p] = mine[:, p * rows : (p + 1) * rows, :].reshape(nx * rows, width).astype(BF16)

    def send_x(off, carry):
        to = lax.rem(gx + off, ci)
        pltpu.make_async_remote_copy(
            x_out.at[to], x_in.at[gx], send.at[3], recv.at[3], device_id=(to, gy, gz), device_id_type=MESH
        ).start()
        return carry

    lax.fori_loop(1, ci, send_x, 0)
    x_in[gx] = x_out[gx]
    wait_bytes(x_in.at[pl.ds(0, ci - 1)], recv.at[3])

    mid[...] = jnp.zeros_like(mid)

    def down(i, carry):
        block = x_in[i].astype(F32).reshape(nx, rows, width)
        acc = mid[...]
        for x in range(nx):
            acc = acc + key_x[:, pl.ds(i * nx + x, 1), :] * block[x][None]
        mid[...] = acc
        return carry

    lax.fori_loop(0, ci, down, 0)

    def up(off, carry):
        to = lax.rem(gx + off, ci)
        line = [jnp.sum(query_x[:, pl.ds(to * nx + x, 1), :] * mid[...], axis=0) for x in range(nx)]
        back_out[to] = jnp.concatenate(line, axis=0).astype(BF16)
        return carry

    def up_send(off, carry):
        up(off, carry)
        to = lax.rem(gx + off, ci)
        pltpu.make_async_remote_copy(
            back_out.at[to],
            back_in.at[gx],
            send.at[4],
            back_recv.at[gx],
            device_id=(to, gy, gz),
            device_id_type=MESH,
        ).start()
        return carry

    lax.fori_loop(1, ci, up_send, 0)
    up(0, 0)
    back_in[gx] = back_out[gx]

    def to_cores(src, lane, chunk):
        for off in range(1, ck):
            pltpu.make_async_remote_copy(
                src,
                gathered.at[lane, chunk],
                send.at[5],
                recv.at[5],
                device_id=(gx, gy, lax.rem(gz + off, ck)),
                device_id_type=MESH,
            ).start()

    def forward(chunk):
        for off in range(1, cj):
            pltpu.make_async_remote_copy(
                back_in.at[chunk],
                gathered.at[lane_of, chunk],
                send.at[5],
                cross_recv.at[gy, chunk],
                device_id=(gx, lax.rem(gy + off, cj), gz),
                device_id_type=MESH,
            ).start()
        to_cores(back_in.at[chunk], lane_of, chunk)
        gathered[lane_of, chunk] = back_in[chunk]

    def relay(chunk):
        for off in range(1, cj):
            j = lax.rem(gy + off, cj)
            lane = j * ck + gz
            wait_bytes(gathered.at[lane, chunk], cross_recv.at[j, chunk])
            to_cores(gathered.at[lane, chunk], lane, chunk)

    forward(gx)

    def arrive(off, carry):
        chunk = lax.rem(gx + ci - off, ci)
        wait_bytes(back_in.at[chunk], back_recv.at[chunk])
        forward(chunk)
        return carry

    lax.fori_loop(1, ci, arrive, 0)

    def pass_on(off, carry):
        relay(lax.rem(gx + ci - off, ci))
        return carry

    lax.fori_loop(0, ci, pass_on, 0)
    if ck > 1:
        wait_bytes(gathered.at[pl.ds(0, cj * (ck - 1))], recv.at[5])
    for g in range(group):
        for q in range(ci):
            at = (g * ci + q) * rows
            out_ref[:, at : at + rows, :] = gathered[g, q].astype(F32).reshape(nx, rows, width)

    wait_bytes(give.at[pl.ds(0, count - 1)], send.at[0])
    wait_bytes(spread.at[pl.ds(0, count - 1)], send.at[1])
    wait_bytes(part_in.at[pl.ds(0, group - 1)], send.at[2])
    wait_bytes(x_out.at[pl.ds(0, ci - 1)], send.at[3])
    wait_bytes(back_out.at[pl.ds(0, ci - 1)], send.at[4])
    wait_bytes(gathered.at[pl.ds(0, group - 1)], send.at[5])


def twice_gelu_times(x, up):
    scale = math.sqrt(2.0 / math.pi)
    tanh = jnp.tanh(x * (x * x * jnp.array(scale * 0.044715, x.dtype) + jnp.array(scale, x.dtype)))
    both = x * up
    return both * tanh + both


def finish_kernel(
    lines, coef_ref, in_ref, tok_ref, wo_ref, wgu_ref, wd_ref, out_ref, query_y, query_z, mixed
):
    _, ny, nz, width = tok_ref.shape
    rank = width // HEADS
    ff = wd_ref.shape[0]

    @pl.when(pl.program_id(0) == 0)
    def _():
        gy, gz = lax.axis_index("gy"), lax.axis_index("gz")
        rows_y = pl.ds(pl.multiple_of(lines[0] + gy * ny, 8), ny)
        rows_z = pl.ds(pl.multiple_of(lines[0] + lines[1] + gz * nz, 8), nz)
        spread_lanes(coef_ref[rows_y, :width], query_y, rank)
        query_z[...] = coef_ref[rows_z, :width].astype(BF16)

    mask = jnp.broadcast_to(jnp.where(head_mask(width, rank), 1.0, 0.0), (HEADS, rank, width)).astype(BF16)
    state = in_ref[0].reshape(rank, rank, width)
    avg = averaging(width)
    twice_avg = jnp.concatenate([avg, avg], axis=0)
    for y in range(0, ny, 2):
        wide = []
        for e in range(2):
            line = jnp.sum(query_y[:, y + e : y + e + 1, :] * state, axis=0).astype(BF16)
            wide.append((mask * line[None]).reshape(HEADS * rank, width))
        pair = dot(query_z[...], jnp.concatenate(wide, axis=1)).astype(BF16)
        mixed[y] = pair[:, :width]
        mixed[y + 1] = pair[:, width:]
    group = ny
    for g in range(0, ny, group):
        rows = group * nz
        tok = tok_ref[0, g : g + group].reshape(rows, width).astype(F32)
        resid = tok + dot(mixed[g : g + group].reshape(rows, width), wo_ref[...])
        high = resid.astype(BF16)
        low = (resid - high.astype(F32)).astype(BF16)
        cent = resid - dot(jnp.concatenate([high, low], axis=1), twice_avg)
        var = dot((cent * cent).astype(BF16), avg)
        inner = (cent * lax.rsqrt(var + EPS)).astype(BF16)
        gate = dot(inner, wgu_ref[:, :ff]).astype(BF16)
        up = dot(inner, wgu_ref[:, ff:]).astype(BF16)
        result = resid + 0.5 * dot(twice_gelu_times(gate, up), wd_ref[...])
        out_ref[0, g : g + group] = result.astype(BF16).reshape(group, nz, width)


def whole(shape):
    return pl.BlockSpec(shape, lambda i: (0,) * len(shape))


def slab(shape):
    return pl.BlockSpec((1,) + shape[1:], lambda i: (i,) + (0,) * (len(shape) - 1))


def params(**more):
    return pltpu.CompilerParams(vmem_limit_bytes=VMEM_LIMIT, **more)


def body(tokens, w_qkv, w_out, w_gate_up, w_down):
    nx, ny, nz, width = tokens.shape
    rank = width // HEADS
    lines = (nx * lax.axis_size("gx"), ny * lax.axis_size("gy"), nz * lax.axis_size("gz"))
    total = sum(lines)
    sizes = tuple(lax.axis_size(a) for a in ("gx", "gy", "gz"))
    count, group = math.prod(sizes), sizes[1] * sizes[2]
    held = -(-nx // group) - (-ny // (sizes[0] * sizes[2])) - (-nz // (sizes[0] * sizes[1]))
    held = -(-held // 8) * 8
    share = rank // group
    rows = share * rank // sizes[0]
    small = (nx, rank * rank, width)
    state, coef = pl.pallas_call(
        functools.partial(attend_kernel, sizes, lines),
        in_specs=[pl.BlockSpec(memory_space=pltpu.VMEM)] * 2,
        out_specs=[pl.BlockSpec(memory_space=pltpu.VMEM)] * 2,
        out_shape=[
            jax.ShapeDtypeStruct(small, F32),
            jax.ShapeDtypeStruct((total, 2 * width), F32),
        ],
        scratch_shapes=[
            pltpu.VMEM(tokens.shape, BF16),
            pltpu.VMEM((nx, width), F32),
            pltpu.VMEM((ny, width), F32),
            pltpu.VMEM((nz, width), F32),
            pltpu.VMEM((count, held, width), F32),
            pltpu.VMEM((count, held, width), F32),
            pltpu.VMEM((held, width), F32),
            pltpu.VMEM((count, held, width), F32),
            pltpu.VMEM((total, width), F32),
            pltpu.VMEM((rank, ny, width), F32),
            pltpu.VMEM((width, nz), BF16),
            pltpu.VMEM((ny, rank, width), F32),
            pltpu.VMEM((nx, rank, rank, width), BF16),
            pltpu.VMEM((group, nx, share, rank, width), BF16),
            pltpu.VMEM((nx, share * rank, width), F32),
            pltpu.VMEM((sizes[0], nx * rows, width), BF16),
            pltpu.VMEM((sizes[0], nx * rows, width), BF16),
            pltpu.VMEM((rank, lines[0], width), F32),
            pltpu.VMEM((rank, lines[0], width), F32),
            pltpu.VMEM((rank, rows, width), F32),
            pltpu.VMEM((sizes[0], nx * rows, width), BF16),
            pltpu.VMEM((sizes[0], nx * rows, width), BF16),
            pltpu.VMEM((group, sizes[0], nx * rows, width), BF16),
            pltpu.SemaphoreType.DMA((6,)),
            pltpu.SemaphoreType.DMA((6,)),
            pltpu.SemaphoreType.DMA((sizes[0],)),
            pltpu.SemaphoreType.DMA((sizes[1], sizes[0])),
        ],
        compiler_params=params(collective_id=0, has_side_effects=True),
        name="attend",
    )(tokens, w_qkv)

    return pl.pallas_call(
        functools.partial(finish_kernel, lines),
        grid=(nx,),
        in_specs=[
            whole(coef.shape),
            slab(small),
            slab(tokens.shape),
            whole(w_out.shape),
            whole(w_gate_up.shape),
            whole(w_down.shape),
        ],
        out_specs=slab(tokens.shape),
        out_shape=jax.ShapeDtypeStruct(tokens.shape, BF16),
        scratch_shapes=[
            pltpu.VMEM((rank, ny, width), F32),
            pltpu.VMEM((nz, width), BF16),
            pltpu.VMEM((ny, nz, width), BF16),
        ],
        compiler_params=params(),
        name="finish",
    )(coef, state, tokens, w_out, w_gate_up, w_down)


def solution(mesh):
    in_specs = (P("gx", "gy", "gz", None), P(), P(), P(), P())
    out_specs = P("gx", "gy", "gz", None)
    return jax.shard_map(body, mesh=mesh, in_specs=in_specs, out_specs=out_specs, check_vma=False)
```

```python
import functools
import math

import jax
import jax.numpy as jnp
from jax import lax
from jax.experimental import pallas as pl
from jax.experimental.pallas import tpu as pltpu
from jax.sharding import PartitionSpec as P

HEADS = 8
EPS = 1e-05
VMEM_LIMIT = 56 * 1024 * 1024
F32 = jnp.float32
BF16 = jnp.bfloat16


def dot(a, b):
    return jnp.dot(a, b, preferred_element_type=F32)


def averaging(width):
    return jnp.full((width, width), 1.0 / width, BF16)


def head_mask(width, rank):
    shape = (HEADS, 1, width)
    lane = lax.broadcasted_iota(jnp.int32, shape, 2)
    return lane // rank == lax.broadcasted_iota(jnp.int32, shape, 0)


def spread_lanes(coefs, out_refs, rank):
    stacked = jnp.concatenate([c.astype(BF16) for c in coefs], axis=0)
    width = stacked.shape[-1]
    row = lax.broadcasted_iota(jnp.int32, (width, 2 * width), 0)
    lane = lax.broadcasted_iota(jnp.int32, (width, 2 * width), 1)
    same = row // rank == lane % width // rank
    index = row % rank - lane // width
    for d in range(0, rank, 2):
        wide = dot(stacked, jnp.where(same & (index == d), 1.0, 0.0).astype(BF16))
        start = 0
        for coef, out_ref in zip(coefs, out_refs):
            rows = coef.shape[0]
            for e in range(2):
                out_ref[d + e] = wide[start : start + rows, e * width : (e + 1) * width]
            start += rows


def coefficients(lines, pool, w_qk, out_ref):
    width = pool.shape[-1]
    rank = width // HEADS
    both = jnp.dot(pool, w_qk.astype(F32), precision=lax.Precision.HIGHEST)
    start = 0
    for length in lines:
        for part in range(2):
            cut = both[start : start + length, part * width : (part + 1) * width]
            total = jnp.sum(jnp.sum(cut * cut, axis=0, keepdims=True), axis=1, keepdims=True)
            unit = cut * lax.rsqrt(total / (length * width) + 1e-06)
            if part == 0:
                unit = unit * (1.0 / math.sqrt(rank * length))
            out_ref[start : start + length, part * width : (part + 1) * width] = unit
        start += length


MESH = pl.DeviceIdType.MESH


def wait_bytes(view, sem):
    pltpu.make_async_copy(view, view, sem).wait()


def attend_kernel(
    sizes,
    lines,
    tok_ref,
    wqkv_ref,
    out_ref,
    coef_ref,
    value,
    pool_x,
    pool_y,
    pool_z,
    give,
    take,
    owned,
    spread,
    pooled,
    key_y,
    key_z,
    state,
    part_out,
    part_in,
    mine,
    x_out,
    x_in,
    query_x,
    key_x,
    mid,
    back_out,
    back_in,
    gathered,
    send,
    recv,
    back_recv,
    cross_recv,
):
    ci, cj, ck = sizes
    count = ci * cj * ck
    group = cj * ck
    nx, ny, nz, width = tok_ref.shape
    rank = width // HEADS
    gx, gy, gz = (lax.axis_index(a) for a in ("gx", "gy", "gz"))
    me = (gx * cj + gy) * ck + gz
    lane_of = gy * ck + gz

    def place(flat):
        return lax.div(flat, group), lax.rem(lax.div(flat, ck), cj), lax.rem(flat, ck)

    barrier = pltpu.get_barrier_semaphore()

    def greet(off, carry):
        pl.semaphore_signal(
            barrier, inc=1, device_id=place(lax.rem(me + off, count)), device_id_type=MESH
        )
        return carry

    lax.fori_loop(1, count, greet, 0)

    avg = averaging(width)
    pool_y[...] = jnp.zeros_like(pool_y)
    pool_z[...] = jnp.zeros_like(pool_z)
    give[...] = jnp.zeros_like(give)

    piece = ny

    def normalise(x, carry):
        by_y, by_z = [], jnp.zeros((nz, width), F32)
        for y in range(0, ny, piece):
            tok = tok_ref[x, y : y + piece].reshape(piece * nz, width)
            cent = tok.astype(F32) - dot(tok, avg)
            var = dot((cent * cent).astype(BF16), avg)
            normed = (cent * lax.rsqrt(var + EPS)).astype(BF16)
            value[x, y : y + piece] = normed.reshape(piece, nz, width)
            full = normed.astype(F32).reshape(piece, nz, width)
            by_y.append(jnp.sum(full, axis=1))
            by_z = by_z + jnp.sum(full, axis=0)
        by_y = jnp.concatenate(by_y, axis=0)
        pool_x[pl.ds(x, 1), :] = jnp.sum(by_y, axis=0, keepdims=True)
        pool_y[...] += by_y
        pool_z[...] += by_z
        return carry

    lax.fori_loop(0, nx, normalise, 0)

    held_x, held_y, held_z = -(-nx // group), -(-ny // (ci * ck)), -(-nz // (ci * cj))

    def starts(i, j, k):
        return (
            jnp.minimum((j * ck + k) * held_x, nx - held_x),
            jnp.minimum((i * ck + k) * held_y, ny - held_y),
            jnp.minimum((i * cj + j) * held_z, nz - held_z),
        )

    def fill(s, carry):
        at_x, at_y, at_z = starts(*place(s))
        for r in range(held_x):
            give[s, r : r + 1, :] = pool_x[pl.ds(at_x + r, 1), :]
        for r in range(held_y):
            give[s, held_x + r : held_x + r + 1, :] = pool_y[pl.ds(at_y + r, 1), :]
        for r in range(held_z):
            row = held_x + held_y + r
            give[s, row : row + 1, :] = pool_z[pl.ds(at_z + r, 1), :]
        return carry

    lax.fori_loop(0, count, fill, 0, unroll=4)
    pl.semaphore_wait(barrier, count - 1)

    def send_rows(off, carry):
        to = lax.rem(me + off, count)
        pltpu.make_async_remote_copy(
            give.at[to], take.at[me], send.at[0], recv.at[0], device_id=place(to), device_id_type=MESH
        ).start()
        return carry

    lax.fori_loop(1, count, send_rows, 0, unroll=4)
    take[me] = give[me]

    def project(x, carry):
        normed = value[x].reshape(ny * nz, width)
        value[x] = dot(normed, wqkv_ref[:, 2 * width :]).astype(BF16).reshape(ny, nz, width)
        return carry

    lax.fori_loop(0, nx, project, 0)
    wait_bytes(take.at[pl.ds(0, count - 1)], recv.at[0])

    row = lax.broadcasted_iota(jnp.int32, owned.shape, 0)

    def add_rows(s, acc):
        i, j, k = place(s)
        ours = jnp.where(
            row < held_x,
            (i == gx).astype(jnp.int32),
            jnp.where(row < held_x + held_y, (j == gy).astype(jnp.int32), (k == gz).astype(jnp.int32)),
        )
        return acc + jnp.where(ours > 0, take[s], 0.0)

    owned[...] = lax.fori_loop(0, count, add_rows, jnp.zeros(owned.shape, F32), unroll=4)

    def send_owned(off, carry):
        to = lax.rem(me + off, count)
        pltpu.make_async_remote_copy(
            owned, spread.at[me], send.at[1], recv.at[1], device_id=place(to), device_id_type=MESH
        ).start()
        return carry

    lax.fori_loop(1, count, send_owned, 0, unroll=4)
    spread[me] = owned[...]
    wait_bytes(spread.at[pl.ds(0, count - 1)], recv.at[1])

    def unfold(s, carry):
        i, j, k = place(s)
        at_x, at_y, at_z = starts(i, j, k)
        for r in range(held_x):
            pooled[pl.ds(i * nx + at_x + r, 1), :] = spread[s, r : r + 1, :]
        for r in range(held_y):
            pooled[pl.ds(lines[0] + j * ny + at_y + r, 1), :] = spread[s, held_x + r : held_x + r + 1, :]
        for r in range(held_z):
            row = held_x + held_y + r
            pooled[pl.ds(lines[0] + lines[1] + k * nz + at_z + r, 1), :] = spread[s, row : row + 1, :]
        return carry

    lax.fori_loop(0, count, unfold, 0, unroll=4)
    coefficients(lines, pooled[...], wqkv_ref[:, : 2 * width], coef_ref)

    rows_y = pl.ds(pl.multiple_of(lines[0] + gy * ny, 8), ny)
    rows_z = pl.ds(pl.multiple_of(lines[0] + lines[1] + gz * nz, 8), nz)
    line_x = lines[0]
    spread_lanes(
        [coef_ref[:line_x, :width], coef_ref[:line_x, width:], coef_ref[rows_y, width:]],
        [query_x, key_x, key_y],
        rank,
    )
    key_z[...] = coef_ref[rows_z, width:].T.astype(BF16)
    mask = head_mask(width, rank)
    share = rank // group

    def compress(x, carry):
        for y in range(0, ny, 2):
            pair = dot(key_z[...], jnp.concatenate([value[x, y], value[x, y + 1]], axis=1))
            for e in range(2):
                full = pair[:, e * width : (e + 1) * width].reshape(HEADS, rank, width)
                state[y + e] = jnp.sum(jnp.where(mask, full, 0.0), axis=0)
        acc = jnp.zeros((rank, rank, width), F32)
        for y in range(ny):
            acc = acc + key_y[:, y : y + 1, :] * state[y][None, :, :]
        part_out[x] = acc.astype(BF16)

        def send_share(off, carry):
            to = lax.rem(lane_of + off, group)
            pltpu.make_async_remote_copy(
                part_out.at[x, pl.ds(to * share, share)],
                part_in.at[lane_of, x],
                send.at[2],
                recv.at[2],
                device_id=(gx, to // ck, to % ck),
                device_id_type=MESH,
            ).start()
            return carry

        lax.fori_loop(1, group, send_share, 0)
        part_in[lane_of, x] = part_out[x, pl.ds(lane_of * share, share)]
        return carry

    lax.fori_loop(0, nx, compress, 0)
    wait_bytes(part_in.at[pl.ds(0, group - 1)], recv.at[2])

    rows = share * rank // ci
    total = jnp.zeros((nx, share, rank, width), F32)
    for g in range(group):
        total = total + part_in[g].astype(F32)
    mine[...] = total.reshape(nx, share * rank, width)
    for p in range(ci):
        x_out[p] = mine[:, p * rows : (p + 1) * rows, :].reshape(nx * rows, width).astype(BF16)

    def send_x(off, carry):
        to = lax.rem(gx + off, ci)
        pltpu.make_async_remote_copy(
            x_out.at[to], x_in.at[gx], send.at[3], recv.at[3], device_id=(to, gy, gz), device_id_type=MESH
        ).start()
        return carry

    lax.fori_loop(1, ci, send_x, 0)
    x_in[gx] = x_out[gx]
    wait_bytes(x_in.at[pl.ds(0, ci - 1)], recv.at[3])

    mid[...] = jnp.zeros_like(mid)

    def down(i, carry):
        block = x_in[i].astype(F32).reshape(nx, rows, width)
        acc = mid[...]
        for x in range(nx):
            acc = acc + key_x[:, pl.ds(i * nx + x, 1), :] * block[x][None]
        mid[...] = acc
        return carry

    lax.fori_loop(0, ci, down, 0)

    def up(off, carry):
        to = lax.rem(gx + off, ci)
        line = [jnp.sum(query_x[:, pl.ds(to * nx + x, 1), :] * mid[...], axis=0) for x in range(nx)]
        back_out[to] = jnp.concatenate(line, axis=0).astype(BF16)
        return carry

    def up_send(off, carry):
        up(off, carry)
        to = lax.rem(gx + off, ci)
        pltpu.make_async_remote_copy(
            back_out.at[to],
            back_in.at[gx],
            send.at[4],
            back_recv.at[gx],
            device_id=(to, gy, gz),
            device_id_type=MESH,
        ).start()
        return carry

    lax.fori_loop(1, ci, up_send, 0)
    up(0, 0)
    back_in[gx] = back_out[gx]

    def to_cores(src, lane, chunk):
        for off in range(1, ck):
            pltpu.make_async_remote_copy(
                src,
                gathered.at[lane, chunk],
                send.at[5],
                recv.at[5],
                device_id=(gx, gy, lax.rem(gz + off, ck)),
                device_id_type=MESH,
            ).start()

    def forward(chunk):
        for off in range(1, cj):
            pltpu.make_async_remote_copy(
                back_in.at[chunk],
                gathered.at[lane_of, chunk],
                send.at[5],
                cross_recv.at[gy, chunk],
                device_id=(gx, lax.rem(gy + off, cj), gz),
                device_id_type=MESH,
            ).start()
        to_cores(back_in.at[chunk], lane_of, chunk)
        gathered[lane_of, chunk] = back_in[chunk]

    def relay(chunk):
        for off in range(1, cj):
            j = lax.rem(gy + off, cj)
            lane = j * ck + gz
            wait_bytes(gathered.at[lane, chunk], cross_recv.at[j, chunk])
            to_cores(gathered.at[lane, chunk], lane, chunk)

    forward(gx)

    def arrive(off, carry):
        chunk = lax.rem(gx + ci - off, ci)
        wait_bytes(back_in.at[chunk], back_recv.at[chunk])
        forward(chunk)
        return carry

    lax.fori_loop(1, ci, arrive, 0)

    def pass_on(off, carry):
        relay(lax.rem(gx + ci - off, ci))
        return carry

    lax.fori_loop(0, ci, pass_on, 0)
    if ck > 1:
        wait_bytes(gathered.at[pl.ds(0, cj * (ck - 1))], recv.at[5])
    for g in range(group):
        for q in range(ci):
            at = (g * ci + q) * rows
            out_ref[:, at : at + rows, :] = gathered[g, q].astype(F32).reshape(nx, rows, width)

    wait_bytes(give.at[pl.ds(0, count - 1)], send.at[0])
    wait_bytes(spread.at[pl.ds(0, count - 1)], send.at[1])
    wait_bytes(part_in.at[pl.ds(0, group - 1)], send.at[2])
    wait_bytes(x_out.at[pl.ds(0, ci - 1)], send.at[3])
    wait_bytes(back_out.at[pl.ds(0, ci - 1)], send.at[4])
    wait_bytes(gathered.at[pl.ds(0, group - 1)], send.at[5])


def twice_gelu_times(x, up):
    scale = math.sqrt(2.0 / math.pi)
    tanh = jnp.tanh(x * (x * x * jnp.array(scale * 0.044715, x.dtype) + jnp.array(scale, x.dtype)))
    both = x * up
    return both * tanh + both


def finish_kernel(
    lines, coef_ref, in_ref, tok_ref, wo_ref, wgu_ref, wd_ref, out_ref, query_y, query_z, mixed
):
    held, ny, nz, width = tok_ref.shape
    rank = width // HEADS
    ff = wd_ref.shape[0]

    @pl.when(pl.program_id(0) == 0)
    def _():
        gy, gz = lax.axis_index("gy"), lax.axis_index("gz")
        rows_y = pl.ds(pl.multiple_of(lines[0] + gy * ny, 8), ny)
        rows_z = pl.ds(pl.multiple_of(lines[0] + lines[1] + gz * nz, 8), nz)
        spread_lanes([coef_ref[rows_y, :width]], [query_y], rank)
        query_z[...] = coef_ref[rows_z, :width].astype(BF16)

    mask = jnp.broadcast_to(jnp.where(head_mask(width, rank), 1.0, 0.0), (HEADS, rank, width)).astype(BF16)
    avg = averaging(width)
    twice_avg = jnp.concatenate([avg, avg], axis=0)
    for x in range(held):
        state = in_ref[x].reshape(rank, rank, width)
        for y in range(0, ny, 2):
            wide = []
            for e in range(2):
                line = jnp.sum(query_y[:, y + e : y + e + 1, :] * state, axis=0).astype(BF16)
                wide.append((mask * line[None]).reshape(HEADS * rank, width))
            pair = dot(query_z[...], jnp.concatenate(wide, axis=1)).astype(BF16)
            mixed[x, y] = pair[:, :width]
            mixed[x, y + 1] = pair[:, width:]
    rows = held * ny * nz
    tok = tok_ref[...].reshape(rows, width).astype(F32)
    resid = tok + dot(mixed[...].reshape(rows, width), wo_ref[...])
    high = resid.astype(BF16)
    low = (resid - high.astype(F32)).astype(BF16)
    cent = resid - dot(jnp.concatenate([high, low], axis=1), twice_avg)
    var = dot((cent * cent).astype(BF16), avg)
    inner = (cent * lax.rsqrt(var + EPS)).astype(BF16)
    gate = dot(inner, wgu_ref[:, :ff]).astype(BF16)
    up = dot(inner, wgu_ref[:, ff:]).astype(BF16)
    result = resid + 0.5 * dot(twice_gelu_times(gate, up), wd_ref[...])
    out_ref[...] = result.astype(BF16).reshape(out_ref.shape)


def whole(shape):
    return pl.BlockSpec(shape, lambda i: (0,) * len(shape))


def slab(shape, held):
    return pl.BlockSpec((held,) + shape[1:], lambda i: (i,) + (0,) * (len(shape) - 1))


def params(**more):
    return pltpu.CompilerParams(vmem_limit_bytes=VMEM_LIMIT, **more)


def body(tokens, w_qkv, w_out, w_gate_up, w_down):
    nx, ny, nz, width = tokens.shape
    rank = width // HEADS
    lines = (nx * lax.axis_size("gx"), ny * lax.axis_size("gy"), nz * lax.axis_size("gz"))
    total = sum(lines)
    sizes = tuple(lax.axis_size(a) for a in ("gx", "gy", "gz"))
    count, group = math.prod(sizes), sizes[1] * sizes[2]
    held = -(-nx // group) - (-ny // (sizes[0] * sizes[2])) - (-nz // (sizes[0] * sizes[1]))
    held = -(-held // 8) * 8
    share = rank // group
    rows = share * rank // sizes[0]
    small = (nx, rank * rank, width)
    state, coef = pl.pallas_call(
        functools.partial(attend_kernel, sizes, lines),
        in_specs=[pl.BlockSpec(memory_space=pltpu.VMEM)] * 2,
        out_specs=[pl.BlockSpec(memory_space=pltpu.VMEM)] * 2,
        out_shape=[
            jax.ShapeDtypeStruct(small, F32),
            jax.ShapeDtypeStruct((total, 2 * width), F32),
        ],
        scratch_shapes=[
            pltpu.VMEM(tokens.shape, BF16),
            pltpu.VMEM((nx, width), F32),
            pltpu.VMEM((ny, width), F32),
            pltpu.VMEM((nz, width), F32),
            pltpu.VMEM((count, held, width), F32),
            pltpu.VMEM((count, held, width), F32),
            pltpu.VMEM((held, width), F32),
            pltpu.VMEM((count, held, width), F32),
            pltpu.VMEM((total, width), F32),
            pltpu.VMEM((rank, ny, width), F32),
            pltpu.VMEM((width, nz), BF16),
            pltpu.VMEM((ny, rank, width), F32),
            pltpu.VMEM((nx, rank, rank, width), BF16),
            pltpu.VMEM((group, nx, share, rank, width), BF16),
            pltpu.VMEM((nx, share * rank, width), F32),
            pltpu.VMEM((sizes[0], nx * rows, width), BF16),
            pltpu.VMEM((sizes[0], nx * rows, width), BF16),
            pltpu.VMEM((rank, lines[0], width), F32),
            pltpu.VMEM((rank, lines[0], width), F32),
            pltpu.VMEM((rank, rows, width), F32),
            pltpu.VMEM((sizes[0], nx * rows, width), BF16),
            pltpu.VMEM((sizes[0], nx * rows, width), BF16),
            pltpu.VMEM((group, sizes[0], nx * rows, width), BF16),
            pltpu.SemaphoreType.DMA((6,)),
            pltpu.SemaphoreType.DMA((6,)),
            pltpu.SemaphoreType.DMA((sizes[0],)),
            pltpu.SemaphoreType.DMA((sizes[1], sizes[0])),
        ],
        compiler_params=params(collective_id=0, has_side_effects=True),
        name="attend",
    )(tokens, w_qkv)

    held = 2 if nx % 2 == 0 else 1
    return pl.pallas_call(
        functools.partial(finish_kernel, lines),
        grid=(nx // held,),
        in_specs=[
            whole(coef.shape),
            slab(small, held),
            slab(tokens.shape, held),
            whole(w_out.shape),
            whole(w_gate_up.shape),
            whole(w_down.shape),
        ],
        out_specs=slab(tokens.shape, held),
        out_shape=jax.ShapeDtypeStruct(tokens.shape, BF16),
        scratch_shapes=[
            pltpu.VMEM((rank, ny, width), F32),
            pltpu.VMEM((nz, width), BF16),
            pltpu.VMEM((held, ny, nz, width), BF16),
        ],
        compiler_params=params(),
        name="finish",
    )(coef, state, tokens, w_out, w_gate_up, w_down)


def solution(mesh):
    in_specs = (P("gx", "gy", "gz", None), P(), P(), P(), P())
    out_specs = P("gx", "gy", "gz", None)
    return jax.shard_map(body, mesh=mesh, in_specs=in_specs, out_specs=out_specs, check_vma=False)
```

```python
import functools
import math

import jax
import jax.numpy as jnp
from jax import lax
from jax.experimental import pallas as pl
from jax.experimental.pallas import tpu as pltpu
from jax.sharding import PartitionSpec as P

HEADS = 8
EPS = 1e-05
VMEM_LIMIT = 56 * 1024 * 1024
F32 = jnp.float32
BF16 = jnp.bfloat16


def dot(a, b):
    return jnp.dot(a, b, preferred_element_type=F32)


def averaging(width):
    return jnp.full((width, width), 1.0 / width, BF16)


def head_mask(width, rank):
    shape = (HEADS, 1, width)
    lane = lax.broadcasted_iota(jnp.int32, shape, 2)
    return lane // rank == lax.broadcasted_iota(jnp.int32, shape, 0)


def spread_lanes(coefs, out_refs, rank):
    stacked = jnp.concatenate([c.astype(BF16) for c in coefs], axis=0)
    width = stacked.shape[-1]
    row = lax.broadcasted_iota(jnp.int32, (width, 2 * width), 0)
    lane = lax.broadcasted_iota(jnp.int32, (width, 2 * width), 1)
    same = row // rank == lane % width // rank
    index = row % rank - lane // width
    for d in range(0, rank, 2):
        wide = dot(stacked, jnp.where(same & (index == d), 1.0, 0.0).astype(BF16))
        start = 0
        for coef, out_ref in zip(coefs, out_refs):
            rows = coef.shape[0]
            for e in range(2):
                out_ref[d + e] = wide[start : start + rows, e * width : (e + 1) * width]
            start += rows


def coefficients(lines, pool, w_qk, out_ref):
    width = pool.shape[-1]
    rank = width // HEADS
    both = jnp.dot(pool, w_qk.astype(F32), precision=lax.Precision.HIGHEST)
    start = 0
    for length in lines:
        for part in range(2):
            cut = both[start : start + length, part * width : (part + 1) * width]
            total = jnp.sum(jnp.sum(cut * cut, axis=0, keepdims=True), axis=1, keepdims=True)
            unit = cut * lax.rsqrt(total / (length * width) + 1e-06)
            if part == 0:
                unit = unit * (1.0 / math.sqrt(rank * length))
            out_ref[start : start + length, part * width : (part + 1) * width] = unit
        start += length


MESH = pl.DeviceIdType.MESH


def wait_bytes(view, sem):
    pltpu.make_async_copy(view, view, sem).wait()


def attend_kernel(
    sizes,
    lines,
    tok_ref,
    wqkv_ref,
    out_ref,
    coef_ref,
    value,
    local,
    near,
    give,
    take,
    owned,
    spread,
    pooled,
    key_y,
    key_z,
    state,
    part_out,
    part_in,
    mine,
    x_out,
    x_in,
    query_x,
    key_x,
    mid,
    back_out,
    back_in,
    gathered,
    send,
    recv,
    back_recv,
    cross_recv,
):
    ci, cj, ck = sizes
    group = cj * ck
    nx, ny, nz, width = tok_ref.shape
    padded = give.shape[1]
    rank = width // HEADS
    gx, gy, gz = (lax.axis_index(a) for a in ("gx", "gy", "gz"))
    lane_of = gy * ck + gz

    def in_group(off):
        lane = lax.rem(lane_of + off, group)
        return (gx, lax.div(lane, ck), lax.rem(lane, ck))

    def along_x(off):
        return (lax.rem(gx + off, ci), gy, gz)

    barrier = pltpu.get_barrier_semaphore()
    for off in range(1, group):
        pl.semaphore_signal(barrier, inc=1, device_id=in_group(off), device_id_type=MESH)
    for off in range(1, ci):
        pl.semaphore_signal(barrier, inc=1, device_id=along_x(off), device_id_type=MESH)

    avg = averaging(width)
    local[...] = jnp.zeros_like(local)
    give[...] = jnp.zeros_like(give)

    piece = ny

    def normalise(x, carry):
        by_y, by_z = [], jnp.zeros((nz, width), F32)
        for y in range(0, ny, piece):
            tok = tok_ref[x, y : y + piece].reshape(piece * nz, width)
            cent = tok.astype(F32) - dot(tok, avg)
            var = dot((cent * cent).astype(BF16), avg)
            normed = (cent * lax.rsqrt(var + EPS)).astype(BF16)
            value[x, y : y + piece] = normed.reshape(piece, nz, width)
            full = normed.astype(F32).reshape(piece, nz, width)
            by_y.append(jnp.sum(full, axis=1))
            by_z = by_z + jnp.sum(full, axis=0)
        by_y = jnp.concatenate(by_y, axis=0)
        local[pl.ds(x, 1), :] = jnp.sum(by_y, axis=0, keepdims=True)
        local[nx : nx + ny, :] += by_y
        local[nx + ny :, :] += by_z
        return carry

    lax.fori_loop(0, nx, normalise, 0)

    pl.semaphore_wait(barrier, group - 1 + ci - 1)
    for off in range(1, group):
        pltpu.make_async_remote_copy(
            local, near.at[lane_of], send.at[0], recv.at[0], device_id=in_group(off), device_id_type=MESH
        ).start()
    near[lane_of] = local[...]

    def project(x, carry):
        normed = value[x].reshape(ny * nz, width)
        value[x] = dot(normed, wqkv_ref[:, 2 * width :]).astype(BF16).reshape(ny, nz, width)
        return carry

    lax.fori_loop(0, nx, project, 0)
    wait_bytes(near.at[pl.ds(0, group - 1)], recv.at[0])

    def over(lanes, start, stop):
        return functools.reduce(lambda u, v: u + v, [near[g, start:stop, :] for g in lanes])

    sum_y = [over([j * ck + k for k in range(ck)], nx, nx + ny) for j in range(cj)]
    sum_z = [over([j * ck + k for j in range(cj)], nx + ny, nx + ny + nz) for k in range(ck)]
    pooled[lines[0] : lines[0] + lines[1], :] = jnp.concatenate(sum_y, axis=0)
    pooled[lines[0] + lines[1] :, :] = jnp.concatenate(sum_z, axis=0)

    part_y, part_z = lines[1] // ci, lines[2] // ci
    base_y, base_z = lines[0], lines[0] + lines[1]
    for q in range(ci):
        give[q, :part_y, :] = pooled[base_y + q * part_y : base_y + (q + 1) * part_y, :]
        give[q, part_y : part_y + part_z, :] = pooled[base_z + q * part_z : base_z + (q + 1) * part_z, :]
    for off in range(1, ci):
        to = along_x(off)
        pltpu.make_async_remote_copy(
            give.at[to[0]], take.at[gx], send.at[1], recv.at[1], device_id=to, device_id_type=MESH
        ).start()
    take[gx] = give[gx]
    owned[padded:, :] = over(range(group), 0, nx)
    wait_bytes(take.at[pl.ds(0, ci - 1)], recv.at[1])
    owned[:padded, :] = jnp.sum(take[...], axis=0)
    for off in range(1, ci):
        pltpu.make_async_remote_copy(
            owned, spread.at[gx], send.at[6], recv.at[6], device_id=along_x(off), device_id_type=MESH
        ).start()
    spread[gx] = owned[...]
    wait_bytes(spread.at[pl.ds(0, ci - 1)], recv.at[6])
    for q in range(ci):
        pooled[q * nx : (q + 1) * nx, :] = spread[q, padded:, :]
        pooled[base_y + q * part_y : base_y + (q + 1) * part_y, :] = spread[q, :part_y, :]
        pooled[base_z + q * part_z : base_z + (q + 1) * part_z, :] = spread[q, part_y : part_y + part_z, :]
    coefficients(lines, pooled[...], wqkv_ref[:, : 2 * width], coef_ref)

    rows_y = pl.ds(pl.multiple_of(lines[0] + gy * ny, 8), ny)
    rows_z = pl.ds(pl.multiple_of(lines[0] + lines[1] + gz * nz, 8), nz)
    line_x = lines[0]
    spread_lanes(
        [coef_ref[:line_x, :width], coef_ref[:line_x, width:], coef_ref[rows_y, width:]],
        [query_x, key_x, key_y],
        rank,
    )
    key_z[...] = coef_ref[rows_z, width:].T.astype(BF16)
    mask = head_mask(width, rank)
    share = rank // group

    def compress(x, carry):
        for y in range(0, ny, 2):
            pair = dot(key_z[...], jnp.concatenate([value[x, y], value[x, y + 1]], axis=1))
            for e in range(2):
                full = pair[:, e * width : (e + 1) * width].reshape(HEADS, rank, width)
                state[y + e] = jnp.sum(jnp.where(mask, full, 0.0), axis=0)
        acc = jnp.zeros((rank, rank, width), F32)
        for y in range(ny):
            acc = acc + key_y[:, y : y + 1, :] * state[y][None, :, :]
        part_out[x] = acc.astype(BF16)

        def send_share(off, carry):
            to = lax.rem(lane_of + off, group)
            pltpu.make_async_remote_copy(
                part_out.at[x, pl.ds(to * share, share)],
                part_in.at[lane_of, x],
                send.at[2],
                recv.at[2],
                device_id=(gx, to // ck, to % ck),
                device_id_type=MESH,
            ).start()
            return carry

        lax.fori_loop(1, group, send_share, 0)
        part_in[lane_of, x] = part_out[x, pl.ds(lane_of * share, share)]
        return carry

    lax.fori_loop(0, nx, compress, 0)
    wait_bytes(part_in.at[pl.ds(0, group - 1)], recv.at[2])

    rows = share * rank // ci
    total = jnp.zeros((nx, share, rank, width), F32)
    for g in range(group):
        total = total + part_in[g].astype(F32)
    mine[...] = total.reshape(nx, share * rank, width)
    for p in range(ci):
        x_out[p] = mine[:, p * rows : (p + 1) * rows, :].reshape(nx * rows, width).astype(BF16)

    def send_x(off, carry):
        to = lax.rem(gx + off, ci)
        pltpu.make_async_remote_copy(
            x_out.at[to], x_in.at[gx], send.at[3], recv.at[3], device_id=(to, gy, gz), device_id_type=MESH
        ).start()
        return carry

    lax.fori_loop(1, ci, send_x, 0)
    x_in[gx] = x_out[gx]
    wait_bytes(x_in.at[pl.ds(0, ci - 1)], recv.at[3])

    mid[...] = jnp.zeros_like(mid)

    def down(i, carry):
        block = x_in[i].astype(F32).reshape(nx, rows, width)
        acc = mid[...]
        for x in range(nx):
            acc = acc + key_x[:, pl.ds(i * nx + x, 1), :] * block[x][None]
        mid[...] = acc
        return carry

    lax.fori_loop(0, ci, down, 0)

    def up(off, carry):
        to = lax.rem(gx + off, ci)
        line = [jnp.sum(query_x[:, pl.ds(to * nx + x, 1), :] * mid[...], axis=0) for x in range(nx)]
        back_out[to] = jnp.concatenate(line, axis=0).astype(BF16)
        return carry

    def up_send(off, carry):
        up(off, carry)
        to = lax.rem(gx + off, ci)
        pltpu.make_async_remote_copy(
            back_out.at[to],
            back_in.at[gx],
            send.at[4],
            back_recv.at[gx],
            device_id=(to, gy, gz),
            device_id_type=MESH,
        ).start()
        return carry

    lax.fori_loop(1, ci, up_send, 0)
    up(0, 0)
    back_in[gx] = back_out[gx]

    def to_cores(src, lane, chunk):
        for off in range(1, ck):
            pltpu.make_async_remote_copy(
                src,
                gathered.at[lane, chunk],
                send.at[5],
                recv.at[5],
                device_id=(gx, gy, lax.rem(gz + off, ck)),
                device_id_type=MESH,
            ).start()

    def forward(chunk):
        for off in range(1, cj):
            pltpu.make_async_remote_copy(
                back_in.at[chunk],
                gathered.at[lane_of, chunk],
                send.at[5],
                cross_recv.at[gy, chunk],
                device_id=(gx, lax.rem(gy + off, cj), gz),
                device_id_type=MESH,
            ).start()
        to_cores(back_in.at[chunk], lane_of, chunk)
        gathered[lane_of, chunk] = back_in[chunk]

    def relay(chunk):
        for off in range(1, cj):
            j = lax.rem(gy + off, cj)
            lane = j * ck + gz
            wait_bytes(gathered.at[lane, chunk], cross_recv.at[j, chunk])
            to_cores(gathered.at[lane, chunk], lane, chunk)

    forward(gx)

    def arrive(off, carry):
        chunk = lax.rem(gx + ci - off, ci)
        wait_bytes(back_in.at[chunk], back_recv.at[chunk])
        forward(chunk)
        return carry

    lax.fori_loop(1, ci, arrive, 0)

    def pass_on(off, carry):
        relay(lax.rem(gx + ci - off, ci))
        return carry

    lax.fori_loop(0, ci, pass_on, 0)
    if ck > 1:
        wait_bytes(gathered.at[pl.ds(0, cj * (ck - 1))], recv.at[5])
    for g in range(group):
        for q in range(ci):
            at = (g * ci + q) * rows
            out_ref[:, at : at + rows, :] = gathered[g, q].astype(F32).reshape(nx, rows, width)

    wait_bytes(near.at[pl.ds(0, group - 1)], send.at[0])
    wait_bytes(take.at[pl.ds(0, ci - 1)], send.at[1])
    wait_bytes(spread.at[pl.ds(0, ci - 1)], send.at[6])
    wait_bytes(part_in.at[pl.ds(0, group - 1)], send.at[2])
    wait_bytes(x_out.at[pl.ds(0, ci - 1)], send.at[3])
    wait_bytes(back_out.at[pl.ds(0, ci - 1)], send.at[4])
    wait_bytes(gathered.at[pl.ds(0, group - 1)], send.at[5])


def twice_gelu_times(x, up):
    scale = math.sqrt(2.0 / math.pi)
    tanh = jnp.tanh(x * (x * x * jnp.array(scale * 0.044715, x.dtype) + jnp.array(scale, x.dtype)))
    both = x * up
    return both * tanh + both


def finish_kernel(
    lines, coef_ref, in_ref, tok_ref, wo_ref, wgu_ref, wd_ref, out_ref, query_y, query_z, mixed
):
    held, ny, nz, width = tok_ref.shape
    rank = width // HEADS
    ff = wd_ref.shape[0]

    @pl.when(pl.program_id(0) == 0)
    def _():
        gy, gz = lax.axis_index("gy"), lax.axis_index("gz")
        rows_y = pl.ds(pl.multiple_of(lines[0] + gy * ny, 8), ny)
        rows_z = pl.ds(pl.multiple_of(lines[0] + lines[1] + gz * nz, 8), nz)
        spread_lanes([coef_ref[rows_y, :width]], [query_y], rank)
        query_z[...] = coef_ref[rows_z, :width].astype(BF16)

    mask = jnp.broadcast_to(jnp.where(head_mask(width, rank), 1.0, 0.0), (HEADS, rank, width)).astype(BF16)
    avg = averaging(width)
    twice_avg = jnp.concatenate([avg, avg], axis=0)
    for x in range(held):
        state = in_ref[x].reshape(rank, rank, width)
        for y in range(0, ny, 2):
            wide = []
            for e in range(2):
                line = jnp.sum(query_y[:, y + e : y + e + 1, :] * state, axis=0).astype(BF16)
                wide.append((mask * line[None]).reshape(HEADS * rank, width))
            pair = dot(query_z[...], jnp.concatenate(wide, axis=1)).astype(BF16)
            mixed[x, y] = pair[:, :width]
            mixed[x, y + 1] = pair[:, width:]
    rows = held * ny * nz
    tok = tok_ref[...].reshape(rows, width).astype(F32)
    resid = tok + dot(mixed[...].reshape(rows, width), wo_ref[...])
    high = resid.astype(BF16)
    low = (resid - high.astype(F32)).astype(BF16)
    cent = resid - dot(jnp.concatenate([high, low], axis=1), twice_avg)
    var = dot((cent * cent).astype(BF16), avg)
    inner = (cent * lax.rsqrt(var + EPS)).astype(BF16)
    gate = dot(inner, wgu_ref[:, :ff]).astype(BF16)
    up = dot(inner, wgu_ref[:, ff:]).astype(BF16)
    result = resid + 0.5 * dot(twice_gelu_times(gate, up), wd_ref[...])
    out_ref[...] = result.astype(BF16).reshape(out_ref.shape)


def whole(shape):
    return pl.BlockSpec(shape, lambda i: (0,) * len(shape))


def slab(shape, held):
    return pl.BlockSpec((held,) + shape[1:], lambda i: (i,) + (0,) * (len(shape) - 1))


def params(**more):
    return pltpu.CompilerParams(vmem_limit_bytes=VMEM_LIMIT, **more)


def body(tokens, w_qkv, w_out, w_gate_up, w_down):
    nx, ny, nz, width = tokens.shape
    rank = width // HEADS
    lines = (nx * lax.axis_size("gx"), ny * lax.axis_size("gy"), nz * lax.axis_size("gz"))
    total = sum(lines)
    sizes = tuple(lax.axis_size(a) for a in ("gx", "gy", "gz"))
    group = sizes[1] * sizes[2]
    padded = -(-(lines[1] // sizes[0] + lines[2] // sizes[0]) // 8) * 8
    share = rank // group
    rows = share * rank // sizes[0]
    small = (nx, rank * rank, width)
    state, coef = pl.pallas_call(
        functools.partial(attend_kernel, sizes, lines),
        in_specs=[pl.BlockSpec(memory_space=pltpu.VMEM)] * 2,
        out_specs=[pl.BlockSpec(memory_space=pltpu.VMEM)] * 2,
        out_shape=[
            jax.ShapeDtypeStruct(small, F32),
            jax.ShapeDtypeStruct((total, 2 * width), F32),
        ],
        scratch_shapes=[
            pltpu.VMEM(tokens.shape, BF16),
            pltpu.VMEM((nx + ny + nz, width), F32),
            pltpu.VMEM((group, nx + ny + nz, width), F32),
            pltpu.VMEM((sizes[0], padded, width), F32),
            pltpu.VMEM((sizes[0], padded, width), F32),
            pltpu.VMEM((padded + nx, width), F32),
            pltpu.VMEM((sizes[0], padded + nx, width), F32),
            pltpu.VMEM((total, width), F32),
            pltpu.VMEM((rank, ny, width), F32),
            pltpu.VMEM((width, nz), BF16),
            pltpu.VMEM((ny, rank, width), F32),
            pltpu.VMEM((nx, rank, rank, width), BF16),
            pltpu.VMEM((group, nx, share, rank, width), BF16),
            pltpu.VMEM((nx, share * rank, width), F32),
            pltpu.VMEM((sizes[0], nx * rows, width), BF16),
            pltpu.VMEM((sizes[0], nx * rows, width), BF16),
            pltpu.VMEM((rank, lines[0], width), F32),
            pltpu.VMEM((rank, lines[0], width), F32),
            pltpu.VMEM((rank, rows, width), F32),
            pltpu.VMEM((sizes[0], nx * rows, width), BF16),
            pltpu.VMEM((sizes[0], nx * rows, width), BF16),
            pltpu.VMEM((group, sizes[0], nx * rows, width), BF16),
            pltpu.SemaphoreType.DMA((7,)),
            pltpu.SemaphoreType.DMA((7,)),
            pltpu.SemaphoreType.DMA((sizes[0],)),
            pltpu.SemaphoreType.DMA((sizes[1], sizes[0])),
        ],
        compiler_params=params(collective_id=0, has_side_effects=True),
        name="attend",
    )(tokens, w_qkv)

    held = 2 if nx % 2 == 0 else 1
    return pl.pallas_call(
        functools.partial(finish_kernel, lines),
        grid=(nx // held,),
        in_specs=[
            whole(coef.shape),
            slab(small, held),
            slab(tokens.shape, held),
            whole(w_out.shape),
            whole(w_gate_up.shape),
            whole(w_down.shape),
        ],
        out_specs=slab(tokens.shape, held),
        out_shape=jax.ShapeDtypeStruct(tokens.shape, BF16),
        scratch_shapes=[
            pltpu.VMEM((rank, ny, width), F32),
            pltpu.VMEM((nz, width), BF16),
            pltpu.VMEM((held, ny, nz, width), BF16),
        ],
        compiler_params=params(),
        name="finish",
    )(coef, state, tokens, w_out, w_gate_up, w_down)


def solution(mesh):
    in_specs = (P("gx", "gy", "gz", None), P(), P(), P(), P())
    out_specs = P("gx", "gy", "gz", None)
    return jax.shard_map(body, mesh=mesh, in_specs=in_specs, out_specs=out_specs, check_vma=False)
```

```python
import functools
import math

import jax
import jax.numpy as jnp
from jax import lax
from jax.experimental import pallas as pl
from jax.experimental.pallas import tpu as pltpu
from jax.sharding import PartitionSpec as P

HEADS = 8
EPS = 1e-05
VMEM_LIMIT = 56 * 1024 * 1024
F32 = jnp.float32
BF16 = jnp.bfloat16


def dot(a, b):
    return jnp.dot(a, b, preferred_element_type=F32)


def averaging(width):
    return jnp.full((width, width), 1.0 / width, BF16)


def head_mask(width, rank):
    shape = (HEADS, 1, width)
    lane = lax.broadcasted_iota(jnp.int32, shape, 2)
    return lane // rank == lax.broadcasted_iota(jnp.int32, shape, 0)


def spread_lanes(coefs, out_refs, rank):
    stacked = jnp.concatenate([c.astype(BF16) for c in coefs], axis=0)
    width = stacked.shape[-1]
    row = lax.broadcasted_iota(jnp.int32, (width, 2 * width), 0)
    lane = lax.broadcasted_iota(jnp.int32, (width, 2 * width), 1)
    same = row // rank == lane % width // rank
    index = row % rank - lane // width
    for d in range(0, rank, 2):
        wide = dot(stacked, jnp.where(same & (index == d), 1.0, 0.0).astype(BF16))
        start = 0
        for coef, out_ref in zip(coefs, out_refs):
            rows = coef.shape[0]
            for e in range(2):
                out_ref[d + e] = wide[start : start + rows, e * width : (e + 1) * width]
            start += rows


def coefficients(lines, pool, w_qk, out_ref):
    width = pool.shape[-1]
    rank = width // HEADS
    both = jnp.dot(pool, w_qk.astype(F32), precision=lax.Precision.HIGHEST)
    start = 0
    for length in lines:
        for part in range(2):
            cut = both[start : start + length, part * width : (part + 1) * width]
            total = jnp.sum(jnp.sum(cut * cut, axis=0, keepdims=True), axis=1, keepdims=True)
            unit = cut * lax.rsqrt(total / (length * width) + 1e-06)
            if part == 0:
                unit = unit * (1.0 / math.sqrt(rank * length))
            out_ref[start : start + length, part * width : (part + 1) * width] = unit
        start += length


MESH = pl.DeviceIdType.MESH


def wait_bytes(view, sem):
    pltpu.make_async_copy(view, view, sem).wait()


def attend_kernel(
    sizes,
    lines,
    tok_ref,
    wqkv_ref,
    out_ref,
    coef_ref,
    value,
    local,
    near,
    give,
    take,
    owned,
    spread,
    pooled,
    key_y,
    key_z,
    state,
    part_out,
    part_in,
    mine,
    x_out,
    x_in,
    query_x,
    key_x,
    mid,
    back_out,
    back_in,
    gathered,
    send,
    recv,
    back_recv,
    cross_recv,
):
    ci, cj, ck = sizes
    group = cj * ck
    nx, ny, nz, width = tok_ref.shape
    padded = give.shape[1]
    rank = width // HEADS
    gx, gy, gz = (lax.axis_index(a) for a in ("gx", "gy", "gz"))
    lane_of = gy * ck + gz

    def in_group(off):
        lane = lax.rem(lane_of + off, group)
        return (gx, lax.div(lane, ck), lax.rem(lane, ck))

    def along_x(off):
        return (lax.rem(gx + off, ci), gy, gz)

    barrier = pltpu.get_barrier_semaphore()
    for off in range(1, group):
        pl.semaphore_signal(barrier, inc=1, device_id=in_group(off), device_id_type=MESH)
    for off in range(1, ci):
        pl.semaphore_signal(barrier, inc=1, device_id=along_x(off), device_id_type=MESH)

    avg = averaging(width)
    local[...] = jnp.zeros_like(local)
    give[...] = jnp.zeros_like(give)

    piece = ny

    def normalise(x, carry):
        by_y, by_z = [], jnp.zeros((nz, width), F32)
        for y in range(0, ny, piece):
            tok = tok_ref[x, y : y + piece].reshape(piece * nz, width)
            cent = tok.astype(F32) - dot(tok, avg)
            var = dot((cent * cent).astype(BF16), avg)
            normed = (cent * lax.rsqrt(var + EPS)).astype(BF16)
            value[x, y : y + piece] = normed.reshape(piece, nz, width)
            full = normed.astype(F32).reshape(piece, nz, width)
            by_y.append(jnp.sum(full, axis=1))
            by_z = by_z + jnp.sum(full, axis=0)
        by_y = jnp.concatenate(by_y, axis=0)
        local[pl.ds(x, 1), :] = jnp.sum(by_y, axis=0, keepdims=True)
        local[nx : nx + ny, :] += by_y
        local[nx + ny :, :] += by_z
        return carry

    lax.fori_loop(0, nx, normalise, 0)

    pl.semaphore_wait(barrier, group - 1 + ci - 1)
    for off in range(1, group):
        pltpu.make_async_remote_copy(
            local, near.at[lane_of], send.at[0], recv.at[0], device_id=in_group(off), device_id_type=MESH
        ).start()
    near[lane_of] = local[...]

    def project(x, carry):
        normed = value[x].reshape(ny * nz, width)
        value[x] = dot(normed, wqkv_ref[:, 2 * width :]).astype(BF16).reshape(ny, nz, width)
        return carry

    lax.fori_loop(0, nx, project, 0)
    wait_bytes(near.at[pl.ds(0, group - 1)], recv.at[0])

    def over(lanes, start, stop):
        return functools.reduce(lambda u, v: u + v, [near[g, start:stop, :] for g in lanes])

    sum_y = [over([j * ck + k for k in range(ck)], nx, nx + ny) for j in range(cj)]
    sum_z = [over([j * ck + k for j in range(cj)], nx + ny, nx + ny + nz) for k in range(ck)]
    pooled[lines[0] : lines[0] + lines[1], :] = jnp.concatenate(sum_y, axis=0)
    pooled[lines[0] + lines[1] :, :] = jnp.concatenate(sum_z, axis=0)

    part_y, part_z = lines[1] // ci, lines[2] // ci
    base_y, base_z = lines[0], lines[0] + lines[1]
    for q in range(ci):
        give[q, :part_y, :] = pooled[base_y + q * part_y : base_y + (q + 1) * part_y, :]
        give[q, part_y : part_y + part_z, :] = pooled[base_z + q * part_z : base_z + (q + 1) * part_z, :]
    for off in range(1, ci):
        to = along_x(off)
        pltpu.make_async_remote_copy(
            give.at[to[0]], take.at[gx], send.at[1], recv.at[1], device_id=to, device_id_type=MESH
        ).start()
    take[gx] = give[gx]
    owned[padded:, :] = over(range(group), 0, nx)
    wait_bytes(take.at[pl.ds(0, ci - 1)], recv.at[1])
    owned[:padded, :] = jnp.sum(take[...], axis=0)
    for off in range(1, ci):
        pltpu.make_async_remote_copy(
            owned, spread.at[gx], send.at[6], recv.at[6], device_id=along_x(off), device_id_type=MESH
        ).start()
    spread[gx] = owned[...]
    wait_bytes(spread.at[pl.ds(0, ci - 1)], recv.at[6])
    for q in range(ci):
        pooled[q * nx : (q + 1) * nx, :] = spread[q, padded:, :]
        pooled[base_y + q * part_y : base_y + (q + 1) * part_y, :] = spread[q, :part_y, :]
        pooled[base_z + q * part_z : base_z + (q + 1) * part_z, :] = spread[q, part_y : part_y + part_z, :]
    coefficients(lines, pooled[...], wqkv_ref[:, : 2 * width], coef_ref)

    rows_y = pl.ds(pl.multiple_of(lines[0] + gy * ny, 8), ny)
    rows_z = pl.ds(pl.multiple_of(lines[0] + lines[1] + gz * nz, 8), nz)
    line_x = lines[0]
    spread_lanes(
        [coef_ref[:line_x, :width], coef_ref[:line_x, width:], coef_ref[rows_y, width:]],
        [query_x, key_x, key_y],
        rank,
    )
    key_z[...] = coef_ref[rows_z, width:].T.astype(BF16)
    mask = head_mask(width, rank)
    share = rank // group

    def compress(x, carry):
        for y in range(0, ny, 2):
            pair = dot(key_z[...], jnp.concatenate([value[x, y], value[x, y + 1]], axis=1))
            for e in range(2):
                full = pair[:, e * width : (e + 1) * width].reshape(HEADS, rank, width)
                state[y + e] = jnp.sum(jnp.where(mask, full, 0.0), axis=0)
        half = rank // 2
        for d in range(0, rank, half):
            acc = jnp.zeros((half, rank, width), F32)
            for y in range(ny):
                acc = acc + key_y[d : d + half, y : y + 1, :] * state[y][None, :, :]
            part_out[x, d : d + half] = acc.astype(BF16)

        def send_share(off, carry):
            to = lax.rem(lane_of + off, group)
            pltpu.make_async_remote_copy(
                part_out.at[x, pl.ds(to * share, share)],
                part_in.at[lane_of, x],
                send.at[2],
                recv.at[2],
                device_id=(gx, to // ck, to % ck),
                device_id_type=MESH,
            ).start()
            return carry

        lax.fori_loop(1, group, send_share, 0)
        part_in[lane_of, x] = part_out[x, pl.ds(lane_of * share, share)]
        return carry

    lax.fori_loop(0, nx, compress, 0)
    wait_bytes(part_in.at[pl.ds(0, group - 1)], recv.at[2])

    rows = share * rank // ci
    total = jnp.zeros((nx, share, rank, width), F32)
    for g in range(group):
        total = total + part_in[g].astype(F32)
    mine[...] = total.reshape(nx, share * rank, width)
    for p in range(ci):
        x_out[p] = mine[:, p * rows : (p + 1) * rows, :].reshape(nx * rows, width).astype(BF16)

    def send_x(off, carry):
        to = lax.rem(gx + off, ci)
        pltpu.make_async_remote_copy(
            x_out.at[to], x_in.at[gx], send.at[3], recv.at[3], device_id=(to, gy, gz), device_id_type=MESH
        ).start()
        return carry

    lax.fori_loop(1, ci, send_x, 0)
    x_in[gx] = x_out[gx]
    wait_bytes(x_in.at[pl.ds(0, ci - 1)], recv.at[3])

    mid[...] = jnp.zeros_like(mid)

    def down(i, carry):
        block = x_in[i].astype(F32).reshape(nx, rows, width)
        acc = mid[...]
        for x in range(nx):
            acc = acc + key_x[:, pl.ds(i * nx + x, 1), :] * block[x][None]
        mid[...] = acc
        return carry

    lax.fori_loop(0, ci, down, 0)

    def up(off, carry):
        to = lax.rem(gx + off, ci)
        line = [jnp.sum(query_x[:, pl.ds(to * nx + x, 1), :] * mid[...], axis=0) for x in range(nx)]
        back_out[to] = jnp.concatenate(line, axis=0).astype(BF16)
        return carry

    def up_send(off, carry):
        up(off, carry)
        to = lax.rem(gx + off, ci)
        pltpu.make_async_remote_copy(
            back_out.at[to],
            back_in.at[gx],
            send.at[4],
            back_recv.at[gx],
            device_id=(to, gy, gz),
            device_id_type=MESH,
        ).start()
        return carry

    lax.fori_loop(1, ci, up_send, 0)
    up(0, 0)
    back_in[gx] = back_out[gx]

    def to_cores(src, lane, chunk):
        for off in range(1, ck):
            pltpu.make_async_remote_copy(
                src,
                gathered.at[lane, chunk],
                send.at[5],
                recv.at[5],
                device_id=(gx, gy, lax.rem(gz + off, ck)),
                device_id_type=MESH,
            ).start()

    def forward(chunk):
        for off in range(1, cj):
            pltpu.make_async_remote_copy(
                back_in.at[chunk],
                gathered.at[lane_of, chunk],
                send.at[5],
                cross_recv.at[gy, chunk],
                device_id=(gx, lax.rem(gy + off, cj), gz),
                device_id_type=MESH,
            ).start()
        to_cores(back_in.at[chunk], lane_of, chunk)
        gathered[lane_of, chunk] = back_in[chunk]

    def relay(chunk):
        for off in range(1, cj):
            j = lax.rem(gy + off, cj)
            lane = j * ck + gz
            wait_bytes(gathered.at[lane, chunk], cross_recv.at[j, chunk])
            to_cores(gathered.at[lane, chunk], lane, chunk)

    forward(gx)

    def arrive(off, carry):
        chunk = lax.rem(gx + ci - off, ci)
        wait_bytes(back_in.at[chunk], back_recv.at[chunk])
        forward(chunk)
        return carry

    lax.fori_loop(1, ci, arrive, 0)

    def pass_on(off, carry):
        relay(lax.rem(gx + ci - off, ci))
        return carry

    lax.fori_loop(0, ci, pass_on, 0)
    if ck > 1:
        wait_bytes(gathered.at[pl.ds(0, cj * (ck - 1))], recv.at[5])
    for g in range(group):
        for q in range(ci):
            at = (g * ci + q) * rows
            out_ref[:, at : at + rows, :] = gathered[g, q].astype(F32).reshape(nx, rows, width)

    wait_bytes(near.at[pl.ds(0, group - 1)], send.at[0])
    wait_bytes(take.at[pl.ds(0, ci - 1)], send.at[1])
    wait_bytes(spread.at[pl.ds(0, ci - 1)], send.at[6])
    wait_bytes(part_in.at[pl.ds(0, group - 1)], send.at[2])
    wait_bytes(x_out.at[pl.ds(0, ci - 1)], send.at[3])
    wait_bytes(back_out.at[pl.ds(0, ci - 1)], send.at[4])
    wait_bytes(gathered.at[pl.ds(0, group - 1)], send.at[5])


def twice_gelu_times(x, up):
    scale = math.sqrt(2.0 / math.pi)
    tanh = jnp.tanh(x * (x * x * jnp.array(scale * 0.044715, x.dtype) + jnp.array(scale, x.dtype)))
    both = x * up
    return both * tanh + both


def finish_kernel(
    lines, coef_ref, in_ref, tok_ref, wo_ref, wgu_ref, wd_ref, out_ref, query_y, query_z, mixed
):
    held, ny, nz, width = tok_ref.shape
    rank = width // HEADS
    ff = wd_ref.shape[0]

    @pl.when(pl.program_id(0) == 0)
    def _():
        gy, gz = lax.axis_index("gy"), lax.axis_index("gz")
        rows_y = pl.ds(pl.multiple_of(lines[0] + gy * ny, 8), ny)
        rows_z = pl.ds(pl.multiple_of(lines[0] + lines[1] + gz * nz, 8), nz)
        spread_lanes([coef_ref[rows_y, :width]], [query_y], rank)
        query_z[...] = coef_ref[rows_z, :width].astype(BF16)

    mask = jnp.broadcast_to(jnp.where(head_mask(width, rank), 1.0, 0.0), (HEADS, rank, width)).astype(BF16)
    avg = averaging(width)
    twice_avg = jnp.concatenate([avg, avg], axis=0)
    for x in range(held):
        state = in_ref[x].reshape(rank, rank, width)
        for y in range(0, ny, 2):
            wide = []
            for e in range(2):
                line = jnp.sum(query_y[:, y + e : y + e + 1, :] * state, axis=0).astype(BF16)
                wide.append((mask * line[None]).reshape(HEADS * rank, width))
            pair = dot(query_z[...], jnp.concatenate(wide, axis=1)).astype(BF16)
            mixed[x, y] = pair[:, :width]
            mixed[x, y + 1] = pair[:, width:]
    rows = held * ny * nz
    tok = tok_ref[...].reshape(rows, width).astype(F32)
    resid = tok + dot(mixed[...].reshape(rows, width), wo_ref[...])
    high = resid.astype(BF16)
    low = (resid - high.astype(F32)).astype(BF16)
    cent = resid - dot(jnp.concatenate([high, low], axis=1), twice_avg)
    var = dot((cent * cent).astype(BF16), avg)
    inner = (cent * lax.rsqrt(var + EPS)).astype(BF16)
    gate = dot(inner, wgu_ref[:, :ff]).astype(BF16)
    up = dot(inner, wgu_ref[:, ff:]).astype(BF16)
    result = resid + 0.5 * dot(twice_gelu_times(gate, up), wd_ref[...])
    out_ref[...] = result.astype(BF16).reshape(out_ref.shape)


def whole(shape):
    return pl.BlockSpec(shape, lambda i: (0,) * len(shape))


def slab(shape, held):
    return pl.BlockSpec((held,) + shape[1:], lambda i: (i,) + (0,) * (len(shape) - 1))


def params(**more):
    return pltpu.CompilerParams(vmem_limit_bytes=VMEM_LIMIT, **more)


def body(tokens, w_qkv, w_out, w_gate_up, w_down):
    nx, ny, nz, width = tokens.shape
    rank = width // HEADS
    lines = (nx * lax.axis_size("gx"), ny * lax.axis_size("gy"), nz * lax.axis_size("gz"))
    total = sum(lines)
    sizes = tuple(lax.axis_size(a) for a in ("gx", "gy", "gz"))
    group = sizes[1] * sizes[2]
    padded = -(-(lines[1] // sizes[0] + lines[2] // sizes[0]) // 8) * 8
    share = rank // group
    rows = share * rank // sizes[0]
    small = (nx, rank * rank, width)
    state, coef = pl.pallas_call(
        functools.partial(attend_kernel, sizes, lines),
        in_specs=[pl.BlockSpec(memory_space=pltpu.VMEM)] * 2,
        out_specs=[pl.BlockSpec(memory_space=pltpu.VMEM)] * 2,
        out_shape=[
            jax.ShapeDtypeStruct(small, F32),
            jax.ShapeDtypeStruct((total, 2 * width), F32),
        ],
        scratch_shapes=[
            pltpu.VMEM(tokens.shape, BF16),
            pltpu.VMEM((nx + ny + nz, width), F32),
            pltpu.VMEM((group, nx + ny + nz, width), F32),
            pltpu.VMEM((sizes[0], padded, width), F32),
            pltpu.VMEM((sizes[0], padded, width), F32),
            pltpu.VMEM((padded + nx, width), F32),
            pltpu.VMEM((sizes[0], padded + nx, width), F32),
            pltpu.VMEM((total, width), F32),
            pltpu.VMEM((rank, ny, width), F32),
            pltpu.VMEM((width, nz), BF16),
            pltpu.VMEM((ny, rank, width), F32),
            pltpu.VMEM((nx, rank, rank, width), BF16),
            pltpu.VMEM((group, nx, share, rank, width), BF16),
            pltpu.VMEM((nx, share * rank, width), F32),
            pltpu.VMEM((sizes[0], nx * rows, width), BF16),
            pltpu.VMEM((sizes[0], nx * rows, width), BF16),
            pltpu.VMEM((rank, lines[0], width), F32),
            pltpu.VMEM((rank, lines[0], width), F32),
            pltpu.VMEM((rank, rows, width), F32),
            pltpu.VMEM((sizes[0], nx * rows, width), BF16),
            pltpu.VMEM((sizes[0], nx * rows, width), BF16),
            pltpu.VMEM((group, sizes[0], nx * rows, width), BF16),
            pltpu.SemaphoreType.DMA((7,)),
            pltpu.SemaphoreType.DMA((7,)),
            pltpu.SemaphoreType.DMA((sizes[0],)),
            pltpu.SemaphoreType.DMA((sizes[1], sizes[0])),
        ],
        compiler_params=params(collective_id=0, has_side_effects=True),
        name="attend",
    )(tokens, w_qkv)

    held = math.gcd(nx, 4)
    return pl.pallas_call(
        functools.partial(finish_kernel, lines),
        grid=(nx // held,),
        in_specs=[
            whole(coef.shape),
            slab(small, held),
            slab(tokens.shape, held),
            whole(w_out.shape),
            whole(w_gate_up.shape),
            whole(w_down.shape),
        ],
        out_specs=slab(tokens.shape, held),
        out_shape=jax.ShapeDtypeStruct(tokens.shape, BF16),
        scratch_shapes=[
            pltpu.VMEM((rank, ny, width), F32),
            pltpu.VMEM((nz, width), BF16),
            pltpu.VMEM((held, ny, nz, width), BF16),
        ],
        compiler_params=params(),
        name="finish",
    )(coef, state, tokens, w_out, w_gate_up, w_down)


def solution(mesh):
    in_specs = (P("gx", "gy", "gz", None), P(), P(), P(), P())
    out_specs = P("gx", "gy", "gz", None)
    return jax.shard_map(body, mesh=mesh, in_specs=in_specs, out_specs=out_specs, check_vma=False)
```
